256 devices in a mesh: ha: 64 (over z, y, core), ta: 4 (over x).
Axes of the slice: x: 4, y: 4, z: 8, core: 2. Of those that a mesh axis runs over, the one named last changes fastest.
Arguments:
- features: bfloat16 [32, 448, 224, 192], P('ta', 'ha'), may hold values from -6 to 6
- norm_gain: float32 [192], replicated, may hold values from 0.5 to 1.5
- head_weight: bfloat16 [3, 192, 27], replicated, may hold values from -0.078125 to 0.078125
- head_bias: float32 [3], replicated, may hold values from -0.5 to 0.5
- frame_order: int32 [32], replicated, may hold values from 0 to 31, each once
- patch_weight: bfloat16 [588, 1152], replicated, may hold values from -0.25 to 0.25
- patch_bias: float32 [1152], replicated, may hold values from -3 to 3
- pos_embed: bfloat16 [2048, 1152], P('ha'), may hold values from -3 to 3
- ln_gain: float32 [1152], replicated, may hold values from 0.5 to 1.5
- ln_bias: float32 [1152], replicated, may hold values from -3 to 3
- w_qkv: bfloat16 [1152, 1728], replicated, may hold values from -1.25 to 1.25
- b_qkv: float32 [1728], replicated, may hold values from -3 to 3
- w_out: bfloat16 [576, 1152], replicated, may hold values from -0.25 to 0.25
- b_out: float32 [1152], replicated, may hold values from -3 to 3
Outputs:
- encoded: bfloat16 [32, 2048, 1152], P('ta', 'ha')
The draws below stay inside these ranges and needn't reach their ends.
Inputs may be any that keep to these rules, and one draw needn't show every extreme that they name: `frame_order`: each of the 32 frames appears once.
All inputs are finite; a program needn't handle non-finite values.
Results may differ from the reference program's by a relative error of at most 0.012.
Values may be sent and summed in bfloat16 or wider, within the bound.
A program may use at most 128 MiB of HBM per device.

```python
import jax
import jax.numpy as jnp
from jax import lax

C = 192
EMBED = 1152
HEADS = 8
HD = 72
PATCH = 14
PW = 32
FRAMES = 32
H2 = 448
W2 = 224
TOKF = 2048
PDIM = 588
QW = 576
N_HA = 64


def draw_w_qkv(key, part):
    key = jax.random.fold_in(key, 7)
    total_cols = 3 * HEADS * HD
    base = jnp.clip(jax.random.normal(key, (EMBED, total_cols), jnp.float32), -4.0, 4.0) * EMBED ** (-0.5)
    return base.astype(jnp.bfloat16)


def level_of(own_key, extent, shards, smallest, high):
    loudness = 1.0
    for position, blocks in shards:
        heights = jax.random.uniform(jax.random.fold_in(jax.random.fold_in(own_key, 6), position), (blocks,), jnp.float32, smallest / len(shards), high / len(shards))
        loudness = loudness * jnp.repeat(jnp.exp(heights), extent[position] // blocks).reshape((-1,) + (1,) * (len(extent) - 1 - position))
    return loudness


def gaussian(stream_key, shape, scale, most, pieces=(), held_as=jnp.bfloat16):
    values = scale * jax.random.normal(stream_key, shape, jnp.float32)
    if pieces:
        values = values * level_of(stream_key, shape, pieces, -0.22, 0.18)
    return jnp.clip(values, -most, most).astype(held_as)


def setup_inputs(seed: int = 0) -> dict:
    streams_of = jax.random.split(jax.random.key(seed), 15)
    features = gaussian(streams_of[0], (FRAMES, H2, W2, C), 1.0, 6.0, ((0, 4), (1, 64)))
    norm_gain = jnp.clip(1.0 + 0.1 * jax.random.normal(streams_of[1], (C,), jnp.float32), 0.5, 1.5)
    head_weight = gaussian(streams_of[2], (3, C, 27), (27 * C) ** -0.5, 0.078125)
    head_bias = jnp.clip(jax.random.uniform(streams_of[3], (3,), jnp.float32, -0.5, 0.5), -0.5, 0.5)
    frame_order = jax.random.permutation(streams_of[4], FRAMES).astype(jnp.int32)
    patch_weight = gaussian(streams_of[5], (PDIM, EMBED), PDIM ** -0.5, 0.25)
    patch_bias = gaussian(streams_of[6], (EMBED,), 0.5, 3.0, (), jnp.float32)
    pos_embed = gaussian(streams_of[7], (TOKF, EMBED), 0.5, 3.0, ((0, 64),))
    ln_gain = jnp.clip(1.0 + 0.1 * jax.random.normal(streams_of[8], (EMBED,), jnp.float32), 0.5, 1.5)
    ln_bias = gaussian(streams_of[9], (EMBED,), 0.5, 3.0, (), jnp.float32)
    w_qkv = draw_w_qkv(jax.random.fold_in(streams_of[14], 71), 0)
    b_qkv = gaussian(streams_of[11], (3 * QW,), 0.5, 3.0, (), jnp.float32)
    w_out = gaussian(streams_of[12], (QW, EMBED), QW ** -0.5, 0.25)
    b_out = gaussian(streams_of[13], (EMBED,), 0.5, 3.0, (), jnp.float32)
    return dict(features=features, norm_gain=norm_gain, head_weight=head_weight, head_bias=head_bias, frame_order=frame_order, patch_weight=patch_weight, patch_bias=patch_bias, pos_embed=pos_embed, ln_gain=ln_gain, ln_bias=ln_bias, w_qkv=w_qkv, b_qkv=b_qkv, w_out=w_out, b_out=b_out)


def activate(values, gain):
    widened = values.astype(jnp.float32)
    factor = lax.rsqrt(lax.optimization_barrier(jnp.mean(widened * widened, axis=-1, keepdims=True)) + 1e-06)
    return jax.nn.silu(widened * factor * gain).astype(jnp.bfloat16)

def assemble(taps):
    frame_count, rows_padded, cols_padded, taps_width = taps.shape
    grid = taps.reshape(frame_count, rows_padded, cols_padded, 3, 3, 3)
    inner_rows = rows_padded - 2
    inner_cols = cols_padded - 2
    row_parts = []
    for row_half in range(2):
        col_parts = []
        for col_half in range(2):
            summed = jnp.zeros((frame_count, inner_rows, inner_cols, 3), jnp.float32)
            for row_tap in range(3):
                top_row = 1 + (row_half + row_tap - 1) // 2
                for col_tap in range(3):
                    left_col = 1 + (col_half + col_tap - 1) // 2
                    summed = summed + grid[:, top_row:top_row + inner_rows, left_col:left_col + inner_cols, row_tap, col_tap, :]
            col_parts.append(summed)
        row_parts.append(jnp.stack(col_parts, axis=3))
    joined = jnp.stack(row_parts, axis=2)
    return joined.reshape(frame_count, 2 * inner_rows, 2 * inner_cols, 3)

def layer_norm(values, gain, shift_terms):
    widened = values.astype(jnp.float32)
    centre = lax.optimization_barrier(jnp.mean(widened, axis=-1, keepdims=True))
    spread = lax.optimization_barrier(jnp.mean((widened - centre) * (widened - centre), axis=-1, keepdims=True))
    return ((widened - centre) * lax.rsqrt(spread + 1e-06) * gain + shift_terms).astype(jnp.bfloat16)

def attend_frame(block):
    queries = block[:, 0].astype(jnp.float32)
    keys_all = block[:, 1].astype(jnp.float32)
    values_all = block[:, 2].astype(jnp.float32)
    scores = jnp.einsum('qhd,khd->hqk', queries, keys_all) * HD ** (-0.5)
    highest = lax.optimization_barrier(jnp.max(scores, axis=-1, keepdims=True))
    expo = jnp.exp(scores - highest)
    weights = (expo / lax.optimization_barrier(jnp.sum(expo, axis=-1, keepdims=True))).astype(jnp.bfloat16)
    context = jnp.einsum('hqk,khd->qhd', weights.astype(jnp.float32), values_all)
    return context.reshape(TOKF, QW).astype(jnp.bfloat16)

def reference(features, norm_gain, head_weight, head_bias, frame_order, patch_weight, patch_bias, pos_embed, ln_gain, ln_bias, w_qkv, b_qkv, w_out, b_out):
    channels = features.shape[3]
    padded = jnp.pad(features, ((2, 0), (0, 0), (0, 0), (0, 0)))
    weight_rows = head_weight.reshape(3 * channels, 27)

    def colour(frame):
        window = lax.dynamic_slice_in_dim(padded, frame.astype(jnp.int32), 3, 0)
        acted = activate(window, norm_gain)
        acted = jnp.pad(acted, ((0, 0), (1, 1), (1, 1), (0, 0)))
        stacked = jnp.transpose(acted, (1, 2, 0, 3)).reshape(-1, 3 * channels)
        taps = jnp.dot(stacked, weight_rows, preferred_element_type=jnp.float32)
        taps = taps.reshape(1, H2 + 2, W2 + 2, 27)
        image = assemble(taps)[0] + head_bias
        tiles = image.reshape(N_HA, PATCH, PW, PATCH, 3).transpose(0, 2, 1, 3, 4)
        return tiles.reshape(TOKF, PDIM).astype(jnp.bfloat16)
    pixels = lax.map(colour, jnp.arange(FRAMES).astype(jnp.int32))
    ordered = jnp.take(pixels, frame_order.astype(jnp.int32), axis=0)
    embedded = jnp.dot(ordered.reshape(-1, PDIM), patch_weight, preferred_element_type=jnp.float32).reshape(FRAMES, TOKF, EMBED)
    embedded = (embedded + patch_bias + pos_embed.astype(jnp.float32)).astype(jnp.bfloat16)
    normed = layer_norm(embedded, ln_gain, ln_bias)
    projected = jnp.dot(normed.reshape(-1, EMBED), w_qkv, preferred_element_type=jnp.float32) + b_qkv
    projected = projected.astype(jnp.bfloat16).reshape(FRAMES, TOKF, 3, HEADS, HD)
    context = lax.map(attend_frame, projected)
    result = jnp.dot(context.reshape(-1, QW), w_out, preferred_element_type=jnp.float32).reshape(FRAMES, TOKF, EMBED)
    result = result + b_out + embedded.astype(jnp.float32)
    return result.astype(jnp.bfloat16)
```

```python
import functools

import jax
import jax.numpy as jnp
import numpy as np
from jax import lax
from jax.experimental import pallas as pl
from jax.experimental.pallas import tpu as pltpu
from jax.sharding import PartitionSpec as P

HEADS = 8
HD = 72
MESH = pl.DeviceIdType.MESH
F32 = jnp.float32
BF16 = jnp.bfloat16

P_ORDER = [0, 13] + list(range(1, 13))


def combine_matrix():
    m = np.zeros((256, 224), np.float32)
    for g in range(2):
        for j in range(3):
            shifted = 1 if (g == 0 and j == 0) or (g == 1 and j == 2) else 0
            base = shifted * 128 + g * 64
            for c in range(3):
                for at, p in enumerate(P_ORDER):
                    r, h = divmod(p, 2)
                    for i in range(3):
                        source = r + (h + i - 1) // 2
                        if 0 <= source < 7:
                            m[base + at * 3 + c, source * 32 + 9 * i + 3 * j + c] = 1
                m[base + 48 + c, 6 * 32 + 3 * j + c] = 1
                m[base + 56 + 3 + c, 18 + 3 * j + c] = 1
    return m.astype(jnp.bfloat16)


def column_matrix():
    m = np.zeros((224, 256), np.float32)
    for x in range(7):
        for token in range(32):
            m[x * 32 + token, 7 * token + x] = 1
    return m.astype(jnp.bfloat16)


def place_matrix():
    m = np.zeros((896, 640), np.float32)
    for x in range(7):
        for g in range(2):
            for at, p in enumerate(P_ORDER):
                for c in range(3):
                    m[x * 128 + g * 64 + at * 3 + c, 3 * (14 * p + 2 * x + g) + c] = 1
    return m.astype(jnp.bfloat16)


def greet(peers):
    barrier = pltpu.get_barrier_semaphore()
    for peer in peers:
        pl.semaphore_signal(barrier, inc=1, device_id=peer, device_id_type=MESH)
    pl.semaphore_wait(barrier, len(peers))


def remote(src, dst, send, recv, peer):
    return pltpu.make_async_remote_copy(
        src_ref=src, dst_ref=dst, send_sem=send, recv_sem=recv, device_id=peer, device_id_type=MESH
    )


def patches_kernel(
    x_hbm,
    taps_ref,
    gain_ref,
    bias_ref,
    order_ref,
    combine_ref,
    column_ref,
    place_ref,
    pos_ref,
    own_ref,
    pos_all_ref,
    x_ref,
    w_ref,
    acc,
    vs,
    edn,
    eup,
    vin,
    edn_c,
    eup_c,
    edn_in,
    eup_in,
    grid,
    gathered,
    pos_in,
    x_sem,
    send_sem,
    recv_sem,
):
    s = lax.axis_index("ha")
    t = lax.axis_index("ta")
    z = s // 8
    q = s % 8
    below = lax.rem(s + 1, 64)
    above = lax.rem(s + 63, 64)
    after = lax.rem(t + 1, 4)
    prior = lax.rem(t + 3, 4)

    loads = [pltpu.make_async_copy(x_hbm.at[f], x_ref.at[f], x_sem.at[f]) for f in range(8)]
    for f in [6, 7, 0, 1, 2, 3, 4, 5]:
        loads[f].start()

    ring = [{"ha": s, "ta": lax.rem(t + d, 4)} for d in range(1, 4)]
    column = [{"ha": lax.rem(z + d, 8) * 8 + q, "ta": t} for d in range(1, 8)]
    near = [
        {"ha": below, "ta": t},
        {"ha": above, "ta": t},
        {"ha": below, "ta": after},
        {"ha": above, "ta": after},
        {"ha": below, "ta": prior},
        {"ha": above, "ta": prior},
    ]
    greet(ring + column + near)

    pos_copies = []
    for d in range(7):
        copy = remote(pos_ref, pos_in.at[z], send_sem.at[8 + d], recv_sem.at[8 + d], column[d])
        copy.start()
        pos_copies.append(copy)

    w_ref[...] = jnp.zeros_like(w_ref)
    for tap in range(3):
        w_ref[tap, 0:27, :] = taps_ref[tap].astype(F32)
    acc[...] = jnp.zeros_like(acc)
    weight = w_ref[...].reshape(96, 192).astype(BF16)

    def convolve(f):
        for r in range(7):
            x = x_ref[f, r].astype(F32)
            factor = lax.rsqrt(jnp.sum(x * x, axis=0, keepdims=True) * (1.0 / 192.0) + 1e-06)
            u = x * factor * gain_ref[...]
            a = (u + u * jnp.tanh(u)).astype(BF16)
            res = jnp.dot(weight, a, preferred_element_type=F32)
            rows = pl.ds(r * 32, 32)
            acc[f, rows, 0:224] += res[64:96]
            acc[f + 1, rows, 0:224] += res[32:64]
            acc[f + 2, rows, 0:224] += res[0:32]

    def combine(f):
        total = acc[f]
        high = total.astype(BF16)
        low = (total - high.astype(F32)).astype(BF16)
        m = combine_ref[...]
        y = jnp.dot(m, high, preferred_element_type=F32) + jnp.dot(
            m, low, preferred_element_type=F32
        )
        for g in range(2):
            moved = pltpu.roll(y[128 + 64 * g : 192 + 64 * g], 1 if g == 0 else 255, 1)
            v = y[64 * g : 64 * g + 64] + moved
            vs[f, g] = v[0:48]
            edn[f, g] = v[48:56]
            eup[f, g] = v[56:64]

    def late(i, carry):
        f = i + 6
        pltpu.make_async_copy(x_hbm.at[f], x_ref.at[f], x_sem.at[f]).wait()
        convolve(f)
        return carry

    def early(f, carry):
        pltpu.make_async_copy(x_hbm.at[f], x_ref.at[f], x_sem.at[f]).wait()
        convolve(f)
        return carry

    lax.fori_loop(0, 2, late, 0)
    for f in (8, 9):
        combine(f)
    tail = pl.ds(8, 2)
    body = pl.ds(0, 8)
    halo = [
        remote(vs.at[tail], vin, send_sem.at[0], recv_sem.at[0], {"ha": s, "ta": after}),
        remote(edn.at[tail], edn_c, send_sem.at[1], recv_sem.at[1], near[2]),
        remote(eup.at[tail], eup_c, send_sem.at[2], recv_sem.at[2], near[3]),
        remote(edn.at[body], edn_in, send_sem.at[3], recv_sem.at[3], near[0]),
        remote(eup.at[body], eup_in, send_sem.at[4], recv_sem.at[4], near[1]),
    ]
    for copy in halo[:3]:
        copy.start()
    lax.fori_loop(0, 6, early, 0)

    def combine_one(f, carry):
        combine(f)
        return carry

    lax.fori_loop(0, 8, combine_one, 0)
    for copy in halo[3:]:
        copy.start()

    colour = lax.rem(lax.broadcasted_iota(jnp.int32, (48, 256), 0), 3)
    bias = jnp.where(colour == 0, bias_ref[0], jnp.where(colour == 1, bias_ref[1], bias_ref[2]))
    from_above = s > 0
    from_below = s < 63
    from_prior = t > 0
    for copy in halo:
        copy.wait()

    for f in range(2):
        for g in range(2):
            vs[f, g] += jnp.where(from_prior, vin[f, g], 0.0)
            vs[f, g, 0:8] += jnp.where(from_prior & from_above, edn_c[f, g], 0.0) + jnp.where(
                from_prior & from_below, eup_c[f, g], 0.0
            )

    def pixels(f, carry):
        parts = []
        for g in range(2):
            edge = jnp.where(from_above, edn_in[f, g], 0.0) + jnp.where(
                from_below, eup_in[f, g], 0.0
            )
            v = vs[f, g] + bias
            parts += [v[0:8] + edge, v[8:48], jnp.zeros((16, 256), F32)]
        v = jnp.concatenate(parts, axis=0).astype(BF16)
        cols = lax.dot_general(
            column_ref[...], v, (((1,), (1,)), ((), ())), preferred_element_type=F32
        ).astype(BF16)
        rows = pl.ds(pl.multiple_of(f * 32, 32), 32)
        for x in range(7):
            grid[rows, x * 128 : (x + 1) * 128] = cols[x * 32 : (x + 1) * 32]
        return carry

    lax.fori_loop(0, 8, pixels, 0)
    mine = pl.ds(t * 8, 8)
    gathered[mine] = (
        jnp.dot(grid[...], place_ref[...], preferred_element_type=F32)
        .astype(BF16)
        .reshape(8, 32, 640)
    )
    copies = []
    for d in range(3):
        copy = remote(
            gathered.at[mine], gathered.at[mine], send_sem.at[5 + d], recv_sem.at[5 + d], ring[d]
        )
        copy.start()
        copies.append(copy)
    for copy in pos_copies:
        copy.wait()
    pos_in[z] = pos_ref[...]
    pos_all_ref[...] = pos_in[...]
    for copy in copies:
        copy.wait()
    for j in range(8):
        own_ref[j] = gathered[order_ref[t * 8 + j]]


def patches(features, norm_gain, head_weight, head_bias, frame_order, pos_embed):
    x = jnp.transpose(features, (0, 1, 3, 2))
    taps = jnp.transpose(head_weight, (0, 2, 1))
    gain = jnp.broadcast_to(0.5 * norm_gain[:, None], (192, 224))
    vmem = pl.BlockSpec(memory_space=pltpu.VMEM)
    smem = pl.BlockSpec(memory_space=pltpu.SMEM)
    return pl.pallas_call(
        patches_kernel,
        out_shape=(
            jax.ShapeDtypeStruct((8, 32, 640), BF16),
            jax.ShapeDtypeStruct((8, 32, 1152), BF16),
        ),
        in_specs=[pl.BlockSpec(memory_space=pl.ANY), vmem, vmem, smem, smem, vmem, vmem, vmem, vmem],
        out_specs=(vmem, vmem),
        scratch_shapes=[
            pltpu.VMEM((8, 7, 192, 224), BF16),
            pltpu.VMEM((3, 32, 192), F32),
            pltpu.VMEM((10, 224, 256), F32),
            pltpu.VMEM((10, 2, 48, 256), F32),
            pltpu.VMEM((10, 2, 8, 256), F32),
            pltpu.VMEM((10, 2, 8, 256), F32),
            pltpu.VMEM((2, 2, 48, 256), F32),
            pltpu.VMEM((2, 2, 8, 256), F32),
            pltpu.VMEM((2, 2, 8, 256), F32),
            pltpu.VMEM((8, 2, 8, 256), F32),
            pltpu.VMEM((8, 2, 8, 256), F32),
            pltpu.VMEM((256, 896), BF16),
            pltpu.VMEM((32, 32, 640), BF16),
            pltpu.VMEM((8, 32, 1152), BF16),
            pltpu.SemaphoreType.DMA((8,)),
            pltpu.SemaphoreType.DMA((15,)),
            pltpu.SemaphoreType.DMA((15,)),
        ],
        compiler_params=pltpu.CompilerParams(
            collective_id=0, has_side_effects=True, vmem_limit_bytes=48 * 1024 * 1024
        ),
        name="patches",
    )(
        x,
        taps,
        gain,
        head_bias,
        frame_order,
        combine_matrix(),
        column_matrix(),
        place_matrix(),
        pos_embed,
    )


import math

def layer_norm(values, gain, shift_terms):
    widened = values.astype(jnp.float32)
    centre = jnp.mean(widened, axis=-1, keepdims=True)
    spread = jnp.mean((widened - centre) * (widened - centre), axis=-1, keepdims=True)
    return ((widened - centre) * lax.rsqrt(spread + 1e-06) * gain + shift_terms).astype(
        jnp.bfloat16
    )


def attend(block):
    items = block.shape[1]
    length = block.shape[2]
    split = block.reshape(items, length, 3, HD)
    queries = split[:, :, 0]
    keys_all = split[:, :, 1]
    values_all = split[:, :, 2]
    rows_step = math.gcd(length, 512)

    def one_block(start):
        query_rows = lax.dynamic_slice_in_dim(queries, start, rows_step, 1)
        scores = jnp.einsum(
            "gqd,gkd->gqk", query_rows, keys_all, preferred_element_type=jnp.float32
        ) * HD ** (-0.5)
        highest = jnp.max(scores, axis=-1, keepdims=True)
        expo = jnp.exp(scores - highest)
        weights = (expo / jnp.sum(expo, axis=-1, keepdims=True)).astype(jnp.bfloat16)
        return jnp.einsum(
            "gqk,gkd->gqd", weights, values_all, preferred_element_type=jnp.float32
        ).astype(jnp.bfloat16)

    starts = jnp.arange(length // rows_step, dtype=jnp.int32) * rows_step
    pieces = lax.map(one_block, starts)
    joined = jnp.transpose(pieces, (1, 0, 2, 3)).reshape(items, length, HD)
    return joined[None]


def shards(
    features,
    norm_gain,
    head_weight,
    head_bias,
    frame_order,
    patch_weight,
    patch_bias,
    pos_embed,
    ln_gain,
    ln_bias,
    w_qkv,
    b_qkv,
    w_out,
    b_out,
):
    own, pos_all = patches(features, norm_gain, head_weight, head_bias, frame_order, pos_embed)
    mine = own[:, :, :588]
    frame_count, across, _ = mine.shape
    embedded = jnp.dot(
        mine.reshape(-1, mine.shape[2]), patch_weight, preferred_element_type=jnp.float32
    ).reshape(frame_count, across, -1)
    embedded = (embedded + patch_bias + pos_embed.astype(jnp.float32)).astype(jnp.bfloat16)
    width = embedded.shape[2]
    normed = layer_norm(embedded, ln_gain, ln_bias)
    projected = (
        jnp.dot(normed.reshape(-1, width), w_qkv, preferred_element_type=jnp.float32) + b_qkv
    )
    projected = projected.astype(jnp.bfloat16).reshape(frame_count, across, 3, HEADS, HD)
    slabs = lax.axis_size("ha")
    groups = frame_count * HEADS // slabs
    arranged = jnp.transpose(projected, (0, 3, 1, 2, 4)).reshape(slabs, groups, across, 3 * HD)
    context = attend(lax.all_to_all(arranged, "ha", split_axis=0, concat_axis=2, tiled=True))
    returned = lax.all_to_all(context, "ha", split_axis=2, concat_axis=0, tiled=True)
    merged = (
        returned.reshape(frame_count, HEADS, across, HD)
        .transpose(0, 2, 1, 3)
        .reshape(-1, HEADS * HD)
    )
    result = jnp.dot(merged, w_out, preferred_element_type=jnp.float32).reshape(
        frame_count, across, width
    )
    result = result + b_out + embedded.astype(jnp.float32)
    return result.astype(jnp.bfloat16)


def solution(mesh):
    in_specs = (
        P("ta", "ha", None, None),
        P(),
        P(),
        P(),
        P(),
        P(),
        P(),
        P("ha", None),
        P(),
        P(),
        P(),
        P(),
        P(),
        P(),
    )
    out_specs = P("ta", "ha", None)
    return jax.shard_map(shards, mesh=mesh, in_specs=in_specs, out_specs=out_specs, check_vma=False)
```

```python
import functools

import jax
import jax.numpy as jnp
import numpy as np
from jax import lax
from jax.experimental import pallas as pl
from jax.experimental.pallas import tpu as pltpu
from jax.sharding import PartitionSpec as P

HEADS = 8
HD = 72
MESH = pl.DeviceIdType.MESH
F32 = jnp.float32
BF16 = jnp.bfloat16

P_ORDER = [0, 13] + list(range(1, 13))


def combine_matrix():
    m = np.zeros((256, 224), np.float32)
    for g in range(2):
        for j in range(3):
            shifted = 1 if (g == 0 and j == 0) or (g == 1 and j == 2) else 0
            base = shifted * 128 + g * 64
            for c in range(3):
                for at, p in enumerate(P_ORDER):
                    r, h = divmod(p, 2)
                    for i in range(3):
                        source = r + (h + i - 1) // 2
                        if 0 <= source < 7:
                            m[base + at * 3 + c, source * 32 + 9 * i + 3 * j + c] = 1
                m[base + 48 + c, 6 * 32 + 3 * j + c] = 1
                m[base + 56 + 3 + c, 18 + 3 * j + c] = 1
    return m.astype(jnp.bfloat16)


def column_matrix():
    m = np.zeros((224, 256), np.float32)
    for x in range(7):
        for token in range(32):
            m[x * 32 + token, 7 * token + x] = 1
    return m.astype(jnp.bfloat16)


def place_matrix():
    m = np.zeros((896, 640), np.float32)
    for x in range(7):
        for g in range(2):
            for at, p in enumerate(P_ORDER):
                for c in range(3):
                    m[x * 128 + g * 64 + at * 3 + c, 3 * (14 * p + 2 * x + g) + c] = 1
    return m.astype(jnp.bfloat16)


def greet(peers):
    barrier = pltpu.get_barrier_semaphore()
    for peer in peers:
        pl.semaphore_signal(barrier, inc=1, device_id=peer, device_id_type=MESH)
    pl.semaphore_wait(barrier, len(peers))


def remote(src, dst, send, recv, peer):
    return pltpu.make_async_remote_copy(
        src_ref=src, dst_ref=dst, send_sem=send, recv_sem=recv, device_id=peer, device_id_type=MESH
    )


def patches_kernel(
    x_hbm,
    taps_ref,
    gain_ref,
    bias_ref,
    order_ref,
    combine_ref,
    column_ref,
    place_ref,
    pos_ref,
    own_ref,
    pos_all_ref,
    x_ref,
    w_ref,
    acc,
    vs,
    edn,
    eup,
    vin,
    edn_c,
    eup_c,
    edn_in,
    eup_in,
    grid,
    gathered,
    pos_in,
    x_sem,
    send_sem,
    recv_sem,
):
    s = lax.axis_index("ha")
    t = lax.axis_index("ta")
    z = s // 8
    q = s % 8
    below = lax.rem(s + 1, 64)
    above = lax.rem(s + 63, 64)
    after = lax.rem(t + 1, 4)
    prior = lax.rem(t + 3, 4)

    loads = [pltpu.make_async_copy(x_hbm.at[f], x_ref.at[f], x_sem.at[f]) for f in range(8)]
    for f in [6, 7, 0, 1, 2, 3, 4, 5]:
        loads[f].start()

    ring = [{"ha": s, "ta": lax.rem(t + d, 4)} for d in range(1, 4)]
    column = [{"ha": lax.rem(z + d, 8) * 8 + q, "ta": t} for d in range(1, 8)]
    near = [
        {"ha": below, "ta": t},
        {"ha": above, "ta": t},
        {"ha": below, "ta": after},
        {"ha": above, "ta": after},
        {"ha": below, "ta": prior},
        {"ha": above, "ta": prior},
    ]
    greet(ring + column + near)

    pos_copies = []
    for d in range(7):
        copy = remote(pos_ref, pos_in.at[z], send_sem.at[8 + d], recv_sem.at[8 + d], column[d])
        copy.start()
        pos_copies.append(copy)

    w_ref[...] = jnp.zeros_like(w_ref)
    for tap in range(3):
        w_ref[tap, 0:27, :] = taps_ref[tap].astype(F32)
    acc[...] = jnp.zeros_like(acc)
    weight = w_ref[...].reshape(96, 192).astype(BF16)

    def convolve(f):
        for r in range(7):
            x = x_ref[f, r].astype(F32)
            factor = lax.rsqrt(jnp.sum(x * x, axis=0, keepdims=True) * (1.0 / 192.0) + 1e-06)
            u = x * factor * gain_ref[...]
            a = (u + u * jnp.tanh(u)).astype(BF16)
            res = jnp.dot(weight, a, preferred_element_type=F32)
            rows = pl.ds(r * 32, 32)
            acc[f, rows, 0:224] += res[64:96]
            acc[f + 1, rows, 0:224] += res[32:64]
            acc[f + 2, rows, 0:224] += res[0:32]

    def combine(f):
        total = acc[f]
        high = total.astype(BF16)
        low = (total - high.astype(F32)).astype(BF16)
        m = combine_ref[...]
        y = jnp.dot(m, high, preferred_element_type=F32) + jnp.dot(
            m, low, preferred_element_type=F32
        )
        for g in range(2):
            moved = pltpu.roll(y[128 + 64 * g : 192 + 64 * g], 1 if g == 0 else 255, 1)
            v = y[64 * g : 64 * g + 64] + moved
            vs[f, g] = v[0:48]
            edn[f, g] = v[48:56]
            eup[f, g] = v[56:64]

    def late(i, carry):
        f = i + 6
        pltpu.make_async_copy(x_hbm.at[f], x_ref.at[f], x_sem.at[f]).wait()
        convolve(f)
        return carry

    def early(f, carry):
        pltpu.make_async_copy(x_hbm.at[f], x_ref.at[f], x_sem.at[f]).wait()
        convolve(f)
        return carry

    lax.fori_loop(0, 2, late, 0)
    for f in (8, 9):
        combine(f)
    tail = pl.ds(8, 2)
    body = pl.ds(0, 8)
    halo = [
        remote(vs.at[tail], vin, send_sem.at[0], recv_sem.at[0], {"ha": s, "ta": after}),
        remote(edn.at[tail], edn_c, send_sem.at[1], recv_sem.at[1], near[2]),
        remote(eup.at[tail], eup_c, send_sem.at[2], recv_sem.at[2], near[3]),
        remote(edn.at[body], edn_in, send_sem.at[3], recv_sem.at[3], near[0]),
        remote(eup.at[body], eup_in, send_sem.at[4], recv_sem.at[4], near[1]),
    ]
    for copy in halo[:3]:
        copy.start()
    lax.fori_loop(0, 6, early, 0)

    def combine_one(f, carry):
        combine(f)
        return carry

    lax.fori_loop(0, 8, combine_one, 0)
    for copy in halo[3:]:
        copy.start()

    colour = lax.rem(lax.broadcasted_iota(jnp.int32, (48, 256), 0), 3)
    bias = jnp.where(colour == 0, bias_ref[0], jnp.where(colour == 1, bias_ref[1], bias_ref[2]))
    from_above = s > 0
    from_below = s < 63
    from_prior = t > 0
    for copy in halo:
        copy.wait()

    for f in range(2):
        for g in range(2):
            vs[f, g] += jnp.where(from_prior, vin[f, g], 0.0)
            vs[f, g, 0:8] += jnp.where(from_prior & from_above, edn_c[f, g], 0.0) + jnp.where(
                from_prior & from_below, eup_c[f, g], 0.0
            )

    def pixels(f, carry):
        parts = []
        for g in range(2):
            edge = jnp.where(from_above, edn_in[f, g], 0.0) + jnp.where(
                from_below, eup_in[f, g], 0.0
            )
            v = vs[f, g] + bias
            parts += [v[0:8] + edge, v[8:48], jnp.zeros((16, 256), F32)]
        v = jnp.concatenate(parts, axis=0).astype(BF16)
        cols = lax.dot_general(
            column_ref[...], v, (((1,), (1,)), ((), ())), preferred_element_type=F32
        ).astype(BF16)
        rows = pl.ds(pl.multiple_of(f * 32, 32), 32)
        for x in range(7):
            grid[rows, x * 128 : (x + 1) * 128] = cols[x * 32 : (x + 1) * 32]
        return carry

    lax.fori_loop(0, 8, pixels, 0)
    mine = pl.ds(t * 8, 8)
    gathered[mine] = (
        jnp.dot(grid[...], place_ref[...], preferred_element_type=F32)
        .astype(BF16)
        .reshape(8, 32, 640)
    )
    copies = []
    for d in range(3):
        copy = remote(
            gathered.at[mine], gathered.at[mine], send_sem.at[5 + d], recv_sem.at[5 + d], ring[d]
        )
        copy.start()
        copies.append(copy)
    for copy in pos_copies:
        copy.wait()
    pos_in[z] = pos_ref[...]
    pos_all_ref[...] = pos_in[...]
    for copy in copies:
        copy.wait()
    for j in range(8):
        own_ref[j] = gathered[order_ref[t * 8 + j]]


def patches(features, norm_gain, head_weight, head_bias, frame_order, pos_embed):
    x = jnp.transpose(features, (0, 1, 3, 2))
    taps = jnp.transpose(head_weight, (0, 2, 1))
    gain = jnp.broadcast_to(0.5 * norm_gain[:, None], (192, 224))
    vmem = pl.BlockSpec(memory_space=pltpu.VMEM)
    smem = pl.BlockSpec(memory_space=pltpu.SMEM)
    return pl.pallas_call(
        patches_kernel,
        out_shape=(
            jax.ShapeDtypeStruct((8, 32, 640), BF16),
            jax.ShapeDtypeStruct((8, 32, 1152), BF16),
        ),
        in_specs=[pl.BlockSpec(memory_space=pl.ANY), vmem, vmem, smem, smem, vmem, vmem, vmem, vmem],
        out_specs=(vmem, vmem),
        scratch_shapes=[
            pltpu.VMEM((8, 7, 192, 224), BF16),
            pltpu.VMEM((3, 32, 192), F32),
            pltpu.VMEM((10, 224, 256), F32),
            pltpu.VMEM((10, 2, 48, 256), F32),
            pltpu.VMEM((10, 2, 8, 256), F32),
            pltpu.VMEM((10, 2, 8, 256), F32),
            pltpu.VMEM((2, 2, 48, 256), F32),
            pltpu.VMEM((2, 2, 8, 256), F32),
            pltpu.VMEM((2, 2, 8, 256), F32),
            pltpu.VMEM((8, 2, 8, 256), F32),
            pltpu.VMEM((8, 2, 8, 256), F32),
            pltpu.VMEM((256, 896), BF16),
            pltpu.VMEM((32, 32, 640), BF16),
            pltpu.VMEM((8, 32, 1152), BF16),
            pltpu.SemaphoreType.DMA((8,)),
            pltpu.SemaphoreType.DMA((15,)),
            pltpu.SemaphoreType.DMA((15,)),
        ],
        compiler_params=pltpu.CompilerParams(
            collective_id=0, has_side_effects=True, vmem_limit_bytes=48 * 1024 * 1024
        ),
        name="patches",
    )(
        x,
        taps,
        gain,
        head_bias,
        frame_order,
        combine_matrix(),
        column_matrix(),
        place_matrix(),
        pos_embed,
    )


def block_kernel(
    own_ref,
    pos_all_ref,
    pos_ref,
    pw_hbm,
    pb_hbm,
    lng_hbm,
    lnb_hbm,
    wqkv_hbm,
    bqkv_hbm,
    wout_hbm,
    bout_hbm,
    out_ref,
    pw_ref,
    pb_ref,
    lng_ref,
    lnb_ref,
    wqkv_ref,
    bqkv_ref,
    wout_ref,
    bout_ref,
    x_in,
    resid,
    normed,
    q_out,
    q_in,
    k_all,
    v_all,
    c_out,
    c_in,
    z_out,
    z_in,
    load_sem,
    send_sem,
    recv_sem,
):
    s = lax.axis_index("ha")
    t = lax.axis_index("ta")
    z = s // 8
    q = s % 8
    loads = [
        pltpu.make_async_copy(source, target, load_sem.at[at])
        for at, (source, target) in enumerate(
            [
                (pw_hbm, pw_ref),
                (pb_hbm, pb_ref),
                (lng_hbm, lng_ref),
                (lnb_hbm, lnb_ref),
                (wqkv_hbm, wqkv_ref),
                (bqkv_hbm, bqkv_ref),
                (wout_hbm, wout_ref),
                (bout_hbm, bout_ref),
            ]
        )
    ]
    for load in loads:
        load.start()
    planes = [lax.rem(z + d, 8) for d in range(1, 8)]
    heads = [lax.rem(q + d, 8) for d in range(1, 8)]
    column = [{"ha": plane * 8 + q, "ta": t} for plane in planes]
    cluster = [{"ha": z * 8 + head, "ta": t} for head in heads]
    greet(column + cluster)

    frames = []
    for d in range(7):
        copy = remote(
            own_ref.at[planes[d]], x_in.at[z], send_sem.at[d], recv_sem.at[d], column[d]
        )
        copy.start()
        frames.append(copy)
    x_in[z] = own_ref[z]

    row = lax.broadcasted_iota(jnp.int32, (80, 256), 0)
    for h in range(8):
        q_out[h, 0] = jnp.zeros((80, 256), BF16)
        q_out[h, 1] = jnp.zeros((80, 256), BF16)
        q_out[h, 2] = jnp.where(row == HD, 1.0, 0.0).astype(BF16)
    z_out[...] = jnp.zeros_like(z_out)

    def embed(tokens, positions):
        value = jnp.dot(
            tokens.reshape(256, 640)[:, :588], pw_ref[...], preferred_element_type=F32
        ).reshape(8, 32, 1152)
        return (value + pb_ref[...].reshape(1, 1, 1152) + positions.astype(F32)).astype(BF16)

    for at in (0, 1):
        loads[at].wait()
    resid[...] = embed(own_ref[...], pos_ref[...].reshape(1, 32, 1152)).reshape(256, 1152)
    for at in (2, 3, 5, 4):
        loads[at].wait()
    bias = jnp.transpose(jnp.broadcast_to(bqkv_ref[...], (8, 1728)))[:, 0:1]
    for copy in frames:
        copy.wait()
    value = embed(x_in[...], pos_all_ref[...]).reshape(256, 1152).astype(F32)
    centre = jnp.mean(value, axis=-1, keepdims=True)
    value = value - centre
    spread = jnp.mean(value * value, axis=-1, keepdims=True)
    normed[...] = (value * lax.rsqrt(spread + 1e-06) * lng_ref[...] + lnb_ref[...]).astype(BF16)

    pairs = {}
    for kind in (1, 2, 0):
        rows = slice(kind * 576, kind * 576 + 576)
        made = (
            lax.dot_general(
                wqkv_ref[rows, :], normed[...], (((1,), (1,)), ((), ())), preferred_element_type=F32
            )
            + bias[rows]
        ).astype(F32)
        for h in range(8):
            q_out[h, kind, 0:HD] = made[h * HD : (h + 1) * HD].astype(BF16)
        for d in range(7):
            at = 7 + kind * 7 + d
            copy = remote(
                q_out.at[heads[d], kind],
                q_in.at[q, kind],
                send_sem.at[at],
                recv_sem.at[at],
                cluster[d],
            )
            copy.start()
            pairs[kind, d] = copy
        q_in[q, kind] = q_out[q, kind]

    for d in range(7):
        pairs[1, d].wait()
    for p in range(8):
        k_all[p * 256 : (p + 1) * 256, :] = jnp.transpose(q_in[p, 1].astype(F32)).astype(BF16)
    for d in range(7):
        pairs[2, d].wait()
    for p in range(8):
        v_all[:, p * 256 : (p + 1) * 256] = q_in[p, 2]
    for d in range(7):
        pairs[0, d].wait()

    rate = HD ** (-0.5) * 1.4426950408889634

    def attend(i, carry):
        p = lax.rem(q + 1 + i, 8)
        scores = jnp.dot(k_all[...], q_in[p, 0], preferred_element_type=F32)
        highest = jnp.max(scores, axis=0, keepdims=True)
        weights = jnp.exp2((scores - highest) * rate).astype(BF16)
        mixed = jnp.dot(v_all[...], weights, preferred_element_type=F32)
        c_out[p] = (mixed / mixed[HD : HD + 1]).astype(BF16)

        @pl.when(i < 7)
        def _():
            remote(
                c_out.at[p],
                c_in.at[q],
                send_sem.at[28 + i],
                recv_sem.at[28 + i],
                {"ha": z * 8 + p, "ta": t},
            ).start()

        return carry

    lax.fori_loop(0, 8, attend, 0)
    c_in[q] = c_out[q]
    for d in range(7):
        remote(
            c_out.at[heads[d]], c_in.at[q], send_sem.at[28 + d], recv_sem.at[28 + d], cluster[d]
        ).wait()
    sides = jnp.concatenate([c_in[h, 0:HD].astype(F32) for h in range(8)], axis=0)
    z_out[:, :, 0:576] = jnp.transpose(sides).astype(BF16).reshape(8, 32, 576)
    backs = []
    for d in range(7):
        copy = remote(
            z_out.at[planes[d]], z_in.at[z], send_sem.at[35 + d], recv_sem.at[35 + d], column[d]
        )
        copy.start()
        backs.append(copy)
    z_in[z] = z_out[z]
    loads[6].wait()
    loads[7].wait()
    for copy in backs:
        copy.wait()
    result = jnp.dot(
        z_in[...].reshape(256, 640)[:, :576], wout_ref[...], preferred_element_type=F32
    )
    result = result + bout_ref[...] + resid[...].astype(F32)
    out_ref[...] = result.astype(BF16).reshape(8, 32, 1152)


def block(own, pos_all, pos, patch_weight, patch_bias, ln_gain, ln_bias, w_qkv, b_qkv, w_out, b_out):
    vmem = pl.BlockSpec(memory_space=pltpu.VMEM)
    hbm = pl.BlockSpec(memory_space=pl.ANY)
    return pl.pallas_call(
        block_kernel,
        out_shape=jax.ShapeDtypeStruct((8, 32, 1152), BF16),
        in_specs=[vmem] * 3 + [hbm] * 8,
        out_specs=vmem,
        scratch_shapes=[
            pltpu.VMEM((588, 1152), BF16),
            pltpu.VMEM((1, 1152), F32),
            pltpu.VMEM((1, 1152), F32),
            pltpu.VMEM((1, 1152), F32),
            pltpu.VMEM((1728, 1152), BF16),
            pltpu.VMEM((1, 1728), F32),
            pltpu.VMEM((576, 1152), BF16),
            pltpu.VMEM((1, 1152), F32),
            pltpu.VMEM((8, 32, 640), BF16),
            pltpu.VMEM((256, 1152), BF16),
            pltpu.VMEM((256, 1152), BF16),
            pltpu.VMEM((8, 3, 80, 256), BF16),
            pltpu.VMEM((8, 3, 80, 256), BF16),
            pltpu.VMEM((2048, 80), BF16),
            pltpu.VMEM((80, 2048), BF16),
            pltpu.VMEM((8, 80, 256), BF16),
            pltpu.VMEM((8, 80, 256), BF16),
            pltpu.VMEM((8, 32, 640), BF16),
            pltpu.VMEM((8, 32, 640), BF16),
            pltpu.SemaphoreType.DMA((8,)),
            pltpu.SemaphoreType.DMA((42,)),
            pltpu.SemaphoreType.DMA((42,)),
        ],
        compiler_params=pltpu.CompilerParams(
            collective_id=1, has_side_effects=True, vmem_limit_bytes=56 * 1024 * 1024
        ),
        name="block",
    )(
        own,
        pos_all,
        pos,
        patch_weight,
        patch_bias.reshape(1, -1),
        ln_gain.reshape(1, -1),
        ln_bias.reshape(1, -1),
        w_qkv.T,
        b_qkv.reshape(1, -1),
        w_out,
        b_out.reshape(1, -1),
    )


def shards(
    features,
    norm_gain,
    head_weight,
    head_bias,
    frame_order,
    patch_weight,
    patch_bias,
    pos_embed,
    ln_gain,
    ln_bias,
    w_qkv,
    b_qkv,
    w_out,
    b_out,
):
    own, pos_all = patches(features, norm_gain, head_weight, head_bias, frame_order, pos_embed)
    return block(
        own,
        pos_all,
        pos_embed,
        patch_weight,
        patch_bias,
        ln_gain,
        ln_bias,
        w_qkv,
        b_qkv,
        w_out,
        b_out,
    )


def solution(mesh):
    in_specs = (
        P("ta", "ha", None, None),
        P(),
        P(),
        P(),
        P(),
        P(),
        P(),
        P("ha", None),
        P(),
        P(),
        P(),
        P(),
        P(),
        P(),
    )
    out_specs = P("ta", "ha", None)
    return jax.shard_map(shards, mesh=mesh, in_specs=in_specs, out_specs=out_specs, check_vma=False)
```

```python
import functools

import jax
import jax.numpy as jnp
import numpy as np
from jax import lax
from jax.experimental import pallas as pl
from jax.experimental.pallas import tpu as pltpu
from jax.sharding import PartitionSpec as P

HEADS = 8
HD = 72
MESH = pl.DeviceIdType.MESH
F32 = jnp.float32
BF16 = jnp.bfloat16

P_ORDER = [0, 13] + list(range(1, 13))


def combine_matrix():
    m = np.zeros((256, 224), np.float32)
    for g in range(2):
        for j in range(3):
            shifted = 1 if (g == 0 and j == 0) or (g == 1 and j == 2) else 0
            base = shifted * 128 + g * 64
            for c in range(3):
                for at, p in enumerate(P_ORDER):
                    r, h = divmod(p, 2)
                    for i in range(3):
                        source = r + (h + i - 1) // 2
                        if 0 <= source < 7:
                            m[base + at * 3 + c, source * 32 + 9 * i + 3 * j + c] = 1
                m[base + 48 + c, 6 * 32 + 3 * j + c] = 1
                m[base + 56 + 3 + c, 18 + 3 * j + c] = 1
    return m.astype(jnp.bfloat16)


def column_matrix():
    m = np.zeros((224, 256), np.float32)
    for x in range(7):
        for token in range(32):
            m[x * 32 + token, 7 * token + x] = 1
    return m.astype(jnp.bfloat16)


def place_matrix():
    m = np.zeros((896, 640), np.float32)
    for x in range(7):
        for g in range(2):
            for at, p in enumerate(P_ORDER):
                for c in range(3):
                    m[x * 128 + g * 64 + at * 3 + c, 3 * (14 * p + 2 * x + g) + c] = 1
    return m.astype(jnp.bfloat16)


def greet(peers):
    barrier = pltpu.get_barrier_semaphore()
    for peer in peers:
        pl.semaphore_signal(barrier, inc=1, device_id=peer, device_id_type=MESH)
    pl.semaphore_wait(barrier, len(peers))


def remote(src, dst, send, recv, peer):
    return pltpu.make_async_remote_copy(
        src_ref=src, dst_ref=dst, send_sem=send, recv_sem=recv, device_id=peer, device_id_type=MESH
    )


def kernel(
    x_hbm,
    taps_hbm,
    gain_hbm,
    bias_hbm,
    order_hbm,
    combine_hbm,
    column_hbm,
    place_hbm,
    pos_hbm,
    pw_hbm,
    pb_hbm,
    lng_hbm,
    lnb_hbm,
    wqkv_hbm,
    bqkv_hbm,
    wout_hbm,
    bout_hbm,
    out_ref,
    x_ref,
    taps_ref,
    gain_ref,
    bias_ref,
    order_ref,
    combine_ref,
    column_ref,
    place_ref,
    pos_ref,
    pw_ref,
    pb_ref,
    lng_ref,
    lnb_ref,
    wqkv_ref,
    bqkv_ref,
    wout_ref,
    bout_ref,
    w_ref,
    acc,
    vs,
    edn,
    eup,
    vin,
    edn_c,
    eup_c,
    edn_in,
    eup_in,
    grid,
    gathered,
    pos_in,
    own_ref,
    x_in,
    resid,
    normed,
    q_out,
    q_in,
    k_all,
    v_all,
    c_out,
    c_in,
    z_out,
    z_in,
    x_sem,
    load_sem,
    near_send,
    near_recv,
    ring_send,
    ring_recv,
    pos_send,
    pos_recv,
    send_sem,
    recv_sem,
):
    s = lax.axis_index("ha")
    t = lax.axis_index("ta")
    z = s // 8
    q = s % 8
    below = lax.rem(s + 1, 64)
    above = lax.rem(s + 63, 64)
    after = lax.rem(t + 1, 4)
    prior = lax.rem(t + 3, 4)

    names = [
        "taps",
        "gain",
        "bias",
        "order",
        "combine",
        "column",
        "place",
        "pos",
        "pw",
        "pb",
        "lng",
        "lnb",
        "wqkv",
        "bqkv",
        "wout",
        "bout",
    ]
    sources = [
        (taps_hbm, taps_ref),
        (gain_hbm, gain_ref),
        (bias_hbm, bias_ref),
        (order_hbm, order_ref),
        (combine_hbm, combine_ref),
        (column_hbm, column_ref),
        (place_hbm, place_ref),
        (pos_hbm, pos_ref),
        (pw_hbm, pw_ref),
        (pb_hbm, pb_ref),
        (lng_hbm, lng_ref),
        (lnb_hbm, lnb_ref),
        (wqkv_hbm, wqkv_ref),
        (bqkv_hbm, bqkv_ref),
        (wout_hbm, wout_ref),
        (bout_hbm, bout_ref),
    ]
    loads = {
        name: pltpu.make_async_copy(source, target, load_sem.at[at])
        for at, (name, (source, target)) in enumerate(zip(names, sources))
    }

    def ready(*wanted):
        for name in wanted:
            loads.pop(name).wait()

    loads["taps"].start()
    loads["gain"].start()
    for f in [6, 7, 0, 1, 2, 3, 4, 5]:
        pltpu.make_async_copy(x_hbm.at[f], x_ref.at[f], x_sem.at[f]).start()
    for name in names[2:]:
        loads[name].start()

    planes = [lax.rem(z + d, 8) for d in range(1, 8)]
    heads = [lax.rem(q + d, 8) for d in range(1, 8)]
    ring = [{"ha": s, "ta": lax.rem(t + d, 4)} for d in range(1, 4)]
    column = [{"ha": plane * 8 + q, "ta": t} for plane in planes]
    cluster = [{"ha": z * 8 + head, "ta": t} for head in heads]
    near = [
        {"ha": below, "ta": t},
        {"ha": above, "ta": t},
        {"ha": below, "ta": after},
        {"ha": above, "ta": after},
        {"ha": below, "ta": prior},
        {"ha": above, "ta": prior},
    ]

    w_ref[...] = jnp.zeros_like(w_ref)
    ready("taps", "gain")
    for tap in range(3):
        w_ref[tap, 0:27, :] = taps_ref[tap].astype(F32)
    acc[...] = jnp.zeros_like(acc)
    gain = jnp.transpose(jnp.broadcast_to(0.5 * gain_ref[...].reshape(1, 192), (8, 192)))[:, 0:1]
    weight = w_ref[...].reshape(96, 192).astype(BF16)

    def convolve(f):
        for r in range(7):
            x = x_ref[f, r].astype(F32)
            factor = lax.rsqrt(jnp.sum(x * x, axis=0, keepdims=True) * (1.0 / 192.0) + 1e-06)
            u = x * factor * gain
            a = (u + u * jnp.tanh(u)).astype(BF16)
            res = jnp.dot(weight, a, preferred_element_type=F32)
            rows = pl.ds(r * 32, 32)
            acc[f, rows, 0:224] += res[64:96]
            acc[f + 1, rows, 0:224] += res[32:64]
            acc[f + 2, rows, 0:224] += res[0:32]

    def combine(f):
        total = acc[f]
        high = total.astype(BF16)
        low = (total - high.astype(F32)).astype(BF16)
        m = combine_ref[...]
        y = jnp.dot(m, high, preferred_element_type=F32) + jnp.dot(
            m, low, preferred_element_type=F32
        )
        for g in range(2):
            moved = pltpu.roll(y[128 + 64 * g : 192 + 64 * g], 1 if g == 0 else 255, 1)
            v = y[64 * g : 64 * g + 64] + moved
            vs[f, g] = v[0:48]
            edn[f, g] = v[48:56]
            eup[f, g] = v[56:64]

    def late(i, carry):
        f = i + 6
        pltpu.make_async_copy(x_hbm.at[f], x_ref.at[f], x_sem.at[f]).wait()
        convolve(f)
        return carry

    def early(f, carry):
        pltpu.make_async_copy(x_hbm.at[f], x_ref.at[f], x_sem.at[f]).wait()
        convolve(f)
        return carry

    greet(ring + column + cluster + near)
    ready("pos")
    pos_copies = []
    for d in range(7):
        copy = remote(pos_ref, pos_in.at[z], pos_send.at[d], pos_recv.at[d], column[d])
        copy.start()
        pos_copies.append(copy)
    lax.fori_loop(0, 2, late, 0)
    ready("combine")
    for f in (8, 9):
        combine(f)
    tail = pl.ds(8, 2)
    body = pl.ds(0, 8)
    halo = [
        remote(vs.at[tail], vin, near_send.at[0], near_recv.at[0], {"ha": s, "ta": after}),
        remote(edn.at[tail], edn_c, near_send.at[1], near_recv.at[1], near[2]),
        remote(eup.at[tail], eup_c, near_send.at[2], near_recv.at[2], near[3]),
        remote(edn.at[body], edn_in, near_send.at[3], near_recv.at[3], near[0]),
        remote(eup.at[body], eup_in, near_send.at[4], near_recv.at[4], near[1]),
    ]
    for copy in halo[:3]:
        copy.start()
    lax.fori_loop(0, 6, early, 0)

    def combine_one(f, carry):
        combine(f)
        return carry

    lax.fori_loop(0, 8, combine_one, 0)
    for copy in halo[3:]:
        copy.start()

    ready("bias", "order", "column", "place")
    colour = lax.rem(lax.broadcasted_iota(jnp.int32, (48, 256), 0), 3)
    bias = jnp.where(colour == 0, bias_ref[0], jnp.where(colour == 1, bias_ref[1], bias_ref[2]))
    from_above = s > 0
    from_below = s < 63
    from_prior = t > 0
    for copy in halo:
        copy.wait()

    for f in range(2):
        for g in range(2):
            vs[f, g] += jnp.where(from_prior, vin[f, g], 0.0)
            vs[f, g, 0:8] += jnp.where(from_prior & from_above, edn_c[f, g], 0.0) + jnp.where(
                from_prior & from_below, eup_c[f, g], 0.0
            )

    def pixels(f, carry):
        parts = []
        for g in range(2):
            edge = jnp.where(from_above, edn_in[f, g], 0.0) + jnp.where(
                from_below, eup_in[f, g], 0.0
            )
            v = vs[f, g] + bias
            parts += [v[0:8] + edge, v[8:48], jnp.zeros((16, 256), F32)]
        v = jnp.concatenate(parts, axis=0).astype(BF16)
        cols = lax.dot_general(
            column_ref[...], v, (((1,), (1,)), ((), ())), preferred_element_type=F32
        ).astype(BF16)
        rows = pl.ds(pl.multiple_of(f * 32, 32), 32)
        for x in range(7):
            grid[rows, x * 128 : (x + 1) * 128] = cols[x * 32 : (x + 1) * 32]
        return carry

    lax.fori_loop(0, 8, pixels, 0)
    mine = pl.ds(t * 8, 8)
    gathered[mine] = (
        jnp.dot(grid[...], place_ref[...], preferred_element_type=F32)
        .astype(BF16)
        .reshape(8, 32, 640)
    )
    copies = []
    for d in range(3):
        copy = remote(
            gathered.at[mine], gathered.at[mine], ring_send.at[d], ring_recv.at[d], ring[d]
        )
        copy.start()
        copies.append(copy)
    for copy in copies:
        copy.wait()
    for j in range(8):
        own_ref[j] = gathered[order_ref[t * 8 + j]]

    frames = []
    for d in range(7):
        copy = remote(
            own_ref.at[planes[d]], x_in.at[z], send_sem.at[d], recv_sem.at[d], column[d]
        )
        copy.start()
        frames.append(copy)
    x_in[z] = own_ref[z]

    row = lax.broadcasted_iota(jnp.int32, (80, 256), 0)
    for h in range(8):
        q_out[h, 0] = jnp.zeros((80, 256), BF16)
        q_out[h, 1] = jnp.zeros((80, 256), BF16)
        q_out[h, 2] = jnp.where(row == HD, 1.0, 0.0).astype(BF16)
    z_out[...] = jnp.zeros_like(z_out)

    def embed(tokens, positions):
        value = jnp.dot(
            tokens.reshape(256, 640)[:, :588], pw_ref[...], preferred_element_type=F32
        ).reshape(8, 32, 1152)
        return (value + pb_ref[...].reshape(1, 1, 1152) + positions.astype(F32)).astype(BF16)

    ready("pw", "pb")
    resid[...] = embed(own_ref[...], pos_ref[...].reshape(1, 32, 1152)).reshape(256, 1152)
    ready("lng", "lnb", "bqkv", "wqkv")
    bias = jnp.transpose(jnp.broadcast_to(bqkv_ref[...].reshape(1, 1728), (8, 1728)))[:, 0:1]
    for copy in frames:
        copy.wait()
    for copy in pos_copies:
        copy.wait()
    pos_in[z] = pos_ref[...]
    value = embed(x_in[...], pos_in[...]).reshape(256, 1152).astype(F32)
    centre = jnp.mean(value, axis=-1, keepdims=True)
    value = value - centre
    spread = jnp.mean(value * value, axis=-1, keepdims=True)
    normed[...] = (value * lax.rsqrt(spread + 1e-06) * lng_ref[...].reshape(1, 1152) + lnb_ref[...].reshape(1, 1152)).astype(BF16)

    pairs = {}
    for kind in (1, 2, 0):
        rows = slice(kind * 576, kind * 576 + 576)
        made = (
            lax.dot_general(
                wqkv_ref[rows, :], normed[...], (((1,), (1,)), ((), ())), preferred_element_type=F32
            )
            + bias[rows]
        ).astype(F32)
        for h in range(8):
            q_out[h, kind, 0:HD] = made[h * HD : (h + 1) * HD].astype(BF16)
        for d in range(7):
            at = 7 + kind * 7 + d
            copy = remote(
                q_out.at[heads[d], kind],
                q_in.at[q, kind],
                send_sem.at[at],
                recv_sem.at[at],
                cluster[d],
            )
            copy.start()
            pairs[kind, d] = copy
        q_in[q, kind] = q_out[q, kind]

    for d in range(7):
        pairs[1, d].wait()
    for p in range(8):
        k_all[p * 256 : (p + 1) * 256, :] = jnp.transpose(q_in[p, 1].astype(F32)).astype(BF16)
    for d in range(7):
        pairs[2, d].wait()
    for p in range(8):
        v_all[:, p * 256 : (p + 1) * 256] = q_in[p, 2]
    for d in range(7):
        pairs[0, d].wait()

    rate = HD ** (-0.5) * 1.4426950408889634

    def attend(i, carry):
        p = lax.rem(q + 1 + i, 8)
        scores = jnp.dot(k_all[...], q_in[p, 0], preferred_element_type=F32)
        highest = jnp.max(scores, axis=0, keepdims=True)
        weights = jnp.exp2((scores - highest) * rate).astype(BF16)
        mixed = jnp.dot(v_all[...], weights, preferred_element_type=F32)
        c_out[p] = (mixed / mixed[HD : HD + 1]).astype(BF16)

        @pl.when(i < 7)
        def _():
            remote(
                c_out.at[p],
                c_in.at[q],
                send_sem.at[28 + i],
                recv_sem.at[28 + i],
                {"ha": z * 8 + p, "ta": t},
            ).start()

        return carry

    lax.fori_loop(0, 8, attend, 0)
    c_in[q] = c_out[q]
    for d in range(7):
        remote(
            c_out.at[heads[d]], c_in.at[q], send_sem.at[28 + d], recv_sem.at[28 + d], cluster[d]
        ).wait()
    sides = jnp.concatenate([c_in[h, 0:HD].astype(F32) for h in range(8)], axis=0)
    z_out[:, :, 0:576] = jnp.transpose(sides).astype(BF16).reshape(8, 32, 576)
    backs = []
    for d in range(7):
        copy = remote(
            z_out.at[planes[d]], z_in.at[z], send_sem.at[35 + d], recv_sem.at[35 + d], column[d]
        )
        copy.start()
        backs.append(copy)
    z_in[z] = z_out[z]
    ready("wout", "bout")
    for copy in backs:
        copy.wait()
    result = jnp.dot(
        z_in[...].reshape(256, 640)[:, :576], wout_ref[...], preferred_element_type=F32
    )
    result = result + bout_ref[...].reshape(1, 1152) + resid[...].astype(F32)
    out_ref[...] = result.astype(BF16).reshape(8, 32, 1152)


def shards(
    features,
    norm_gain,
    head_weight,
    head_bias,
    frame_order,
    patch_weight,
    patch_bias,
    pos_embed,
    ln_gain,
    ln_bias,
    w_qkv,
    b_qkv,
    w_out,
    b_out,
):
    hbm = pl.BlockSpec(memory_space=pl.ANY)
    vmem = pl.BlockSpec(memory_space=pltpu.VMEM)
    return pl.pallas_call(
        kernel,
        out_shape=jax.ShapeDtypeStruct((8, 32, 1152), BF16),
        in_specs=[hbm] * 17,
        out_specs=vmem,
        scratch_shapes=[
            pltpu.VMEM((8, 7, 192, 224), BF16),
            pltpu.VMEM((3, 27, 192), BF16),
            pltpu.VMEM((192,), F32),
            pltpu.SMEM((3,), F32),
            pltpu.SMEM((32,), jnp.int32),
            pltpu.VMEM((256, 224), BF16),
            pltpu.VMEM((224, 256), BF16),
            pltpu.VMEM((896, 640), BF16),
            pltpu.VMEM((32, 1152), BF16),
            pltpu.VMEM((588, 1152), BF16),
            pltpu.VMEM((1152,), F32),
            pltpu.VMEM((1152,), F32),
            pltpu.VMEM((1152,), F32),
            pltpu.VMEM((1728, 1152), BF16),
            pltpu.VMEM((1728,), F32),
            pltpu.VMEM((576, 1152), BF16),
            pltpu.VMEM((1152,), F32),
            pltpu.VMEM((3, 32, 192), F32),
            pltpu.VMEM((10, 224, 256), F32),
            pltpu.VMEM((10, 2, 48, 256), F32),
            pltpu.VMEM((10, 2, 8, 256), F32),
            pltpu.VMEM((10, 2, 8, 256), F32),
            pltpu.VMEM((2, 2, 48, 256), F32),
            pltpu.VMEM((2, 2, 8, 256), F32),
            pltpu.VMEM((2, 2, 8, 256), F32),
            pltpu.VMEM((8, 2, 8, 256), F32),
            pltpu.VMEM((8, 2, 8, 256), F32),
            pltpu.VMEM((256, 896), BF16),
            pltpu.VMEM((32, 32, 640), BF16),
            pltpu.VMEM((8, 32, 1152), BF16),
            pltpu.VMEM((8, 32, 640), BF16),
            pltpu.VMEM((8, 32, 640), BF16),
            pltpu.VMEM((256, 1152), BF16),
            pltpu.VMEM((256, 1152), BF16),
            pltpu.VMEM((8, 3, 80, 256), BF16),
            pltpu.VMEM((8, 3, 80, 256), BF16),
            pltpu.VMEM((2048, 80), BF16),
            pltpu.VMEM((80, 2048), BF16),
            pltpu.VMEM((8, 80, 256), BF16),
            pltpu.VMEM((8, 80, 256), BF16),
            pltpu.VMEM((8, 32, 640), BF16),
            pltpu.VMEM((8, 32, 640), BF16),
            pltpu.SemaphoreType.DMA((8,)),
            pltpu.SemaphoreType.DMA((16,)),
            pltpu.SemaphoreType.DMA((5,)),
            pltpu.SemaphoreType.DMA((5,)),
            pltpu.SemaphoreType.DMA((3,)),
            pltpu.SemaphoreType.DMA((3,)),
            pltpu.SemaphoreType.DMA((7,)),
            pltpu.SemaphoreType.DMA((7,)),
            pltpu.SemaphoreType.DMA((42,)),
            pltpu.SemaphoreType.DMA((42,)),
        ],
        compiler_params=pltpu.CompilerParams(
            collective_id=0, has_side_effects=True, vmem_limit_bytes=60 * 1024 * 1024
        ),
        name="decoder_block",
    )(
        jnp.transpose(features, (0, 1, 3, 2)),
        jnp.transpose(head_weight, (0, 2, 1)),
        norm_gain,
        head_bias,
        frame_order,
        combine_matrix(),
        column_matrix(),
        place_matrix(),
        pos_embed,
        patch_weight,
        patch_bias,
        ln_gain,
        ln_bias,
        w_qkv.T,
        b_qkv,
        w_out,
        b_out,
    )


def solution(mesh):
    in_specs = (
        P("ta", "ha", None, None),
        P(),
        P(),
        P(),
        P(),
        P(),
        P(),
        P("ha", None),
        P(),
        P(),
        P(),
        P(),
        P(),
        P(),
    )
    out_specs = P("ta", "ha", None)
    return jax.shard_map(shards, mesh=mesh, in_specs=in_specs, out_specs=out_specs, check_vma=False)
```

```python
import functools

import jax
import jax.numpy as jnp
import numpy as np
from jax import lax
from jax.experimental import pallas as pl
from jax.experimental.pallas import tpu as pltpu
from jax.sharding import PartitionSpec as P

HEADS = 8
HD = 72
MESH = pl.DeviceIdType.MESH
F32 = jnp.float32
BF16 = jnp.bfloat16

P_ORDER = [0, 13] + list(range(1, 13))


def combine_matrix():
    m = np.zeros((256, 224), np.float32)
    for g in range(2):
        for j in range(3):
            shifted = 1 if (g == 0 and j == 0) or (g == 1 and j == 2) else 0
            base = shifted * 128 + g * 64
            for c in range(3):
                for at, p in enumerate(P_ORDER):
                    r, h = divmod(p, 2)
                    for i in range(3):
                        source = r + (h + i - 1) // 2
                        if 0 <= source < 7:
                            m[base + at * 3 + c, source * 32 + 9 * i + 3 * j + c] = 1
                m[base + 48 + c, 6 * 32 + 3 * j + c] = 1
                m[base + 56 + 3 + c, 18 + 3 * j + c] = 1
    return m.astype(jnp.bfloat16)


def column_matrix():
    m = np.zeros((224, 256), np.float32)
    for x in range(7):
        for token in range(32):
            m[x * 32 + token, 7 * token + x] = 1
    return m.astype(jnp.bfloat16)


def order_matrix():
    m = np.zeros((640, 588), np.float32)
    for q in range(14):
        for at, p in enumerate(P_ORDER):
            for c in range(3):
                m[q * 42 + at * 3 + c, 3 * (14 * p + q) + c] = 1
    return m.astype(jnp.bfloat16)


def remote(src, dst, send, recv, peer):
    return pltpu.make_async_remote_copy(
        src_ref=src, dst_ref=dst, send_sem=send, recv_sem=recv, device_id=peer, device_id_type=MESH
    )


def kernel(
    x_hbm,
    taps_hbm,
    gain_hbm,
    bias_hbm,
    order_hbm,
    combine_hbm,
    column_hbm,
    perm_hbm,
    pos_hbm,
    pw_hbm,
    pb_hbm,
    lng_hbm,
    lnb_hbm,
    wqkv_hbm,
    bqkv_hbm,
    wout_hbm,
    bout_hbm,
    out_ref,
    x_ref,
    taps_ref,
    gain_ref,
    bias_ref,
    order_ref,
    combine_ref,
    column_ref,
    perm_ref,
    pos_ref,
    pw_ref,
    pb_ref,
    lng_ref,
    lnb_ref,
    wqkv_ref,
    bqkv_ref,
    wout_ref,
    bout_ref,
    w_ref,
    acc,
    vs,
    edn,
    eup,
    vin,
    edn_c,
    eup_c,
    edn_in,
    eup_in,
    pw_all,
    gathered,
    pos_in,
    own_ref,
    x_in,
    resid,
    normed,
    q_out,
    q_in,
    k_all,
    v_all,
    c_out,
    c_in,
    z_out,
    z_in,
    x_sem,
    load_sem,
    near_send,
    near_recv,
    edge_send,
    edge_recv,
    ring_send,
    ring_recv,
    pos_send,
    pos_recv,
    send_sem,
    recv_sem,
):
    s = lax.axis_index("ha")
    t = lax.axis_index("ta")
    z = s // 8
    q = s % 8
    below = lax.rem(s + 1, 64)
    above = lax.rem(s + 63, 64)
    after = lax.rem(t + 1, 4)
    prior = lax.rem(t + 3, 4)

    names = [
        "taps",
        "gain",
        "bias",
        "order",
        "combine",
        "column",
        "perm",
        "pos",
        "pw",
        "pb",
        "lng",
        "lnb",
        "wqkv",
        "bqkv",
        "wout",
        "bout",
    ]
    sources = [
        (taps_hbm, taps_ref),
        (gain_hbm, gain_ref),
        (bias_hbm, bias_ref),
        (order_hbm, order_ref),
        (combine_hbm, combine_ref),
        (column_hbm, column_ref),
        (perm_hbm, perm_ref),
        (pos_hbm, pos_ref),
        (pw_hbm, pw_ref),
        (pb_hbm, pb_ref),
        (lng_hbm, lng_ref),
        (lnb_hbm, lnb_ref),
        (wqkv_hbm, wqkv_ref),
        (bqkv_hbm, bqkv_ref),
        (wout_hbm, wout_ref),
        (bout_hbm, bout_ref),
    ]
    loads = {
        name: pltpu.make_async_copy(source, target, load_sem.at[at])
        for at, (name, (source, target)) in enumerate(zip(names, sources))
    }

    def ready(*wanted):
        for name in wanted:
            loads.pop(name).wait()

    loads["taps"].start()
    loads["gain"].start()
    for f in [6, 7, 0, 1, 2, 3, 4, 5]:
        pltpu.make_async_copy(x_hbm.at[f], x_ref.at[f], x_sem.at[f]).start()
    for name in names[2:]:
        loads[name].start()

    planes = [lax.rem(z + d, 8) for d in range(1, 8)]
    heads = [lax.rem(q + d, 8) for d in range(1, 8)]
    ring = [{"ha": s, "ta": lax.rem(t + d, 4)} for d in range(1, 4)]
    column = [{"ha": plane * 8 + q, "ta": t} for plane in planes]
    cluster = [{"ha": z * 8 + head, "ta": t} for head in heads]
    near = [
        {"ha": below, "ta": t},
        {"ha": above, "ta": t},
        {"ha": below, "ta": after},
        {"ha": above, "ta": after},
        {"ha": below, "ta": prior},
        {"ha": above, "ta": prior},
    ]

    peers = ring + column + cluster + near
    barrier = pltpu.get_barrier_semaphore()
    for peer in peers:
        pl.semaphore_signal(barrier, inc=1, device_id=peer, device_id_type=MESH)

    w_ref[...] = jnp.zeros_like(w_ref)
    ready("taps", "gain")
    for tap in range(3):
        w_ref[tap, 0:27, :] = taps_ref[tap].astype(F32)
    acc[...] = jnp.zeros_like(acc)
    gain = jnp.transpose(jnp.broadcast_to(0.5 * gain_ref[...].reshape(1, 192), (8, 192)))[:, 0:1]
    weight = w_ref[...].reshape(96, 192).astype(BF16)

    def convolve(f):
        for r in range(7):
            x = x_ref[f, r].astype(F32)
            factor = lax.rsqrt(jnp.sum(x * x, axis=0, keepdims=True) * (1.0 / 192.0) + 1e-06)
            u = x * factor * gain
            a = (u + u * jnp.tanh(u)).astype(BF16)
            res = jnp.dot(weight, a, preferred_element_type=F32)
            rows = pl.ds(r * 32, 32)
            acc[f, rows, 0:224] += res[64:96]
            acc[f + 1, rows, 0:224] += res[32:64]
            acc[f + 2, rows, 0:224] += res[0:32]

    def combine(f):
        total = acc[f]
        high = total.astype(BF16)
        low = (total - high.astype(F32)).astype(BF16)
        m = combine_ref[...]
        y = jnp.dot(m, high, preferred_element_type=F32) + jnp.dot(
            m, low, preferred_element_type=F32
        )
        for g in range(2):
            moved = pltpu.roll(y[128 + 64 * g : 192 + 64 * g], 1 if g == 0 else 255, 1)
            v = y[64 * g : 64 * g + 64] + moved
            vs[f, g] = v[0:48]
            edn[f, g] = v[48:56]
            eup[f, g] = v[56:64]

    def late(i, carry):
        f = i + 6
        pltpu.make_async_copy(x_hbm.at[f], x_ref.at[f], x_sem.at[f]).wait()
        convolve(f)
        return carry

    colour = lax.rem(lax.broadcasted_iota(jnp.int32, (48, 256), 0), 3)
    from_above = s > 0
    from_below = s < 63
    from_prior = t > 0

    def edges(f):
        return [
            remote(edn.at[f], edn_in.at[f], edge_send.at[0, f], edge_recv.at[0, f], near[0]),
            remote(eup.at[f], eup_in.at[f], edge_send.at[1, f], edge_recv.at[1, f], near[1]),
        ]

    def spread(f):
        slot = t * 8 + f
        return [
            remote(
                gathered.at[slot],
                gathered.at[slot],
                ring_send.at[d, f],
                ring_recv.at[d, f],
                ring[d],
            )
            for d in range(3)
        ]

    def finish(f):
        for copy in edges(f):
            copy.wait()
        bias = jnp.where(colour == 0, bias_ref[0], jnp.where(colour == 1, bias_ref[1], bias_ref[2]))
        parts = []
        for g in range(2):
            edge = jnp.where(from_above, edn_in[f, g], 0.0) + jnp.where(
                from_below, eup_in[f, g], 0.0
            )
            v = vs[f, g] + bias
            parts += [v[0:8] + edge, v[8:48], jnp.zeros((16, 256), F32)]
        v = jnp.concatenate(parts, axis=0).astype(BF16)
        cols = lax.dot_general(
            column_ref[...], v, (((1,), (1,)), ((), ())), preferred_element_type=F32
        )
        pieces = [
            cols[x * 32 : (x + 1) * 32, g * 64 : g * 64 + 42] for x in range(7) for g in range(2)
        ]
        pieces.append(jnp.zeros((32, 52), F32))
        gathered[t * 8 + f] = jnp.concatenate(pieces, axis=1).astype(BF16)
        for copy in spread(f):
            copy.start()

    lax.fori_loop(0, 2, late, 0)
    pl.semaphore_wait(barrier, len(peers))
    ready("combine")
    for f in (8, 9):
        combine(f)
    tail = pl.ds(8, 2)
    halo = [
        remote(vs.at[tail], vin, near_send.at[0], near_recv.at[0], {"ha": s, "ta": after}),
        remote(edn.at[tail], edn_c, near_send.at[1], near_recv.at[1], near[2]),
        remote(eup.at[tail], eup_c, near_send.at[2], near_recv.at[2], near[3]),
    ]
    for copy in halo:
        copy.start()
    ready("pos", "bias", "column")
    pos_copies = []
    for d in range(7):
        copy = remote(pos_ref, pos_in.at[z], pos_send.at[d], pos_recv.at[d], column[d])
        copy.start()
        pos_copies.append(copy)

    def early(f, carry):
        pltpu.make_async_copy(x_hbm.at[f], x_ref.at[f], x_sem.at[f]).wait()
        convolve(f)
        combine(f)
        for copy in edges(f):
            copy.start()

        @pl.when(f == 1)
        def _():
            for copy in halo:
                copy.wait()
            for first in range(2):
                for g in range(2):
                    extra = jnp.where(from_prior, vin[first, g], 0.0)
                    corner = jnp.where(from_prior & from_above, edn_c[first, g], 0.0) + jnp.where(
                        from_prior & from_below, eup_c[first, g], 0.0
                    )
                    vs[first, g] += extra
                    vs[first, g, 0:8] += corner

        @pl.when(f > 0)
        def _():
            finish(f - 1)

        return carry

    lax.fori_loop(0, 6, early, 0)
    for f in (6, 7):
        combine(f)
        for copy in edges(f):
            copy.start()
    lax.fori_loop(5, 8, lambda f, carry: (finish(f), carry)[1], 0)
    ready("perm", "pw", "order")
    pw_all[...] = jnp.dot(perm_ref[...], pw_ref[...], preferred_element_type=F32).astype(BF16)
    for f in range(8):
        for copy in spread(f):
            copy.wait()
    for j in range(8):
        own_ref[j] = gathered[order_ref[t * 8 + j]]

    frames = []
    for d in range(7):
        copy = remote(
            own_ref.at[planes[d]], x_in.at[z], send_sem.at[d], recv_sem.at[d], column[d]
        )
        copy.start()
        frames.append(copy)
    x_in[z] = own_ref[z]

    row = lax.broadcasted_iota(jnp.int32, (80, 256), 0)
    for h in range(8):
        q_out[h, 0] = jnp.zeros((80, 256), BF16)
        q_out[h, 1] = jnp.zeros((80, 256), BF16)
        q_out[h, 2] = jnp.where(row == HD, 1.0, 0.0).astype(BF16)
    z_out[...] = jnp.zeros_like(z_out)

    def embed(tokens, positions):
        value = jnp.dot(
            tokens.reshape(256, 640), pw_all[...], preferred_element_type=F32
        ).reshape(8, 32, 1152)
        return (value + pb_ref[...].reshape(1, 1, 1152) + positions.astype(F32)).astype(BF16)

    ready("pb")
    resid[...] = embed(own_ref[...], pos_ref[...].reshape(1, 32, 1152)).reshape(256, 1152)
    ready("lng", "lnb", "bqkv", "wqkv")
    bias = jnp.transpose(jnp.broadcast_to(bqkv_ref[...].reshape(1, 1728), (8, 1728)))[:, 0:1]
    for copy in frames:
        copy.wait()
    for copy in pos_copies:
        copy.wait()
    pos_in[z] = pos_ref[...]
    value = embed(x_in[...], pos_in[...]).reshape(256, 1152).astype(F32)
    centre = jnp.mean(value, axis=-1, keepdims=True)
    value = value - centre
    spread = jnp.mean(value * value, axis=-1, keepdims=True)
    normed[...] = (value * lax.rsqrt(spread + 1e-06) * lng_ref[...].reshape(1, 1152) + lnb_ref[...].reshape(1, 1152)).astype(BF16)

    pairs = {}
    for kind in (1, 2, 0):
        rows = slice(kind * 576, kind * 576 + 576)
        made = (
            lax.dot_general(
                wqkv_ref[rows, :], normed[...], (((1,), (1,)), ((), ())), preferred_element_type=F32
            )
            + bias[rows]
        ).astype(F32)
        for h in range(8):
            q_out[h, kind, 0:HD] = made[h * HD : (h + 1) * HD].astype(BF16)
        for d in range(7):
            at = 7 + kind * 7 + d
            copy = remote(
                q_out.at[heads[d], kind],
                q_in.at[q, kind],
                send_sem.at[at],
                recv_sem.at[at],
                cluster[d],
            )
            copy.start()
            pairs[kind, d] = copy
        q_in[q, kind] = q_out[q, kind]

    for d in range(7):
        pairs[1, d].wait()
    for p in range(8):
        k_all[p * 256 : (p + 1) * 256, :] = jnp.transpose(q_in[p, 1].astype(F32)).astype(BF16)
    for d in range(7):
        pairs[2, d].wait()
    for p in range(8):
        v_all[:, p * 256 : (p + 1) * 256] = q_in[p, 2]
    for d in range(7):
        pairs[0, d].wait()

    rate = HD ** (-0.5) * 1.4426950408889634

    def attend(i, carry):
        p = lax.rem(q + 1 + i, 8)
        scores = jnp.dot(k_all[...], q_in[p, 0], preferred_element_type=F32)
        highest = jnp.max(scores, axis=0, keepdims=True)
        weights = jnp.exp2((scores - highest) * rate).astype(BF16)
        mixed = jnp.dot(v_all[...], weights, preferred_element_type=F32)
        c_out[p] = (mixed / mixed[HD : HD + 1]).astype(BF16)

        @pl.when(i < 7)
        def _():
            remote(
                c_out.at[p],
                c_in.at[q],
                send_sem.at[28 + i],
                recv_sem.at[28 + i],
                {"ha": z * 8 + p, "ta": t},
            ).start()

        return carry

    lax.fori_loop(0, 8, attend, 0)
    c_in[q] = c_out[q]
    for d in range(7):
        remote(
            c_out.at[heads[d]], c_in.at[q], send_sem.at[28 + d], recv_sem.at[28 + d], cluster[d]
        ).wait()
    sides = jnp.concatenate([c_in[h, 0:HD].astype(F32) for h in range(8)], axis=0)
    z_out[:, :, 0:576] = jnp.transpose(sides).astype(BF16).reshape(8, 32, 576)
    backs = []
    for d in range(7):
        copy = remote(
            z_out.at[planes[d]], z_in.at[z], send_sem.at[35 + d], recv_sem.at[35 + d], column[d]
        )
        copy.start()
        backs.append(copy)
    z_in[z] = z_out[z]
    ready("wout", "bout")
    for copy in backs:
        copy.wait()
    result = jnp.dot(
        z_in[...].reshape(256, 640)[:, :576], wout_ref[...], preferred_element_type=F32
    )
    result = result + bout_ref[...].reshape(1, 1152) + resid[...].astype(F32)
    out_ref[...] = result.astype(BF16).reshape(8, 32, 1152)


def shards(
    features,
    norm_gain,
    head_weight,
    head_bias,
    frame_order,
    patch_weight,
    patch_bias,
    pos_embed,
    ln_gain,
    ln_bias,
    w_qkv,
    b_qkv,
    w_out,
    b_out,
):
    hbm = pl.BlockSpec(memory_space=pl.ANY)
    vmem = pl.BlockSpec(memory_space=pltpu.VMEM)
    return pl.pallas_call(
        kernel,
        out_shape=jax.ShapeDtypeStruct((8, 32, 1152), BF16),
        in_specs=[hbm] * 17,
        out_specs=vmem,
        scratch_shapes=[
            pltpu.VMEM((8, 7, 192, 224), BF16),
            pltpu.VMEM((3, 27, 192), BF16),
            pltpu.VMEM((192,), F32),
            pltpu.SMEM((3,), F32),
            pltpu.SMEM((32,), jnp.int32),
            pltpu.VMEM((256, 224), BF16),
            pltpu.VMEM((224, 256), BF16),
            pltpu.VMEM((640, 588), BF16),
            pltpu.VMEM((32, 1152), BF16),
            pltpu.VMEM((588, 1152), BF16),
            pltpu.VMEM((1152,), F32),
            pltpu.VMEM((1152,), F32),
            pltpu.VMEM((1152,), F32),
            pltpu.VMEM((1728, 1152), BF16),
            pltpu.VMEM((1728,), F32),
            pltpu.VMEM((576, 1152), BF16),
            pltpu.VMEM((1152,), F32),
            pltpu.VMEM((3, 32, 192), F32),
            pltpu.VMEM((10, 224, 256), F32),
            pltpu.VMEM((10, 2, 48, 256), F32),
            pltpu.VMEM((10, 2, 8, 256), F32),
            pltpu.VMEM((10, 2, 8, 256), F32),
            pltpu.VMEM((2, 2, 48, 256), F32),
            pltpu.VMEM((2, 2, 8, 256), F32),
            pltpu.VMEM((2, 2, 8, 256), F32),
            pltpu.VMEM((8, 2, 8, 256), F32),
            pltpu.VMEM((8, 2, 8, 256), F32),
            pltpu.VMEM((640, 1152), BF16),
            pltpu.VMEM((32, 32, 640), BF16),
            pltpu.VMEM((8, 32, 1152), BF16),
            pltpu.VMEM((8, 32, 640), BF16),
            pltpu.VMEM((8, 32, 640), BF16),
            pltpu.VMEM((256, 1152), BF16),
            pltpu.VMEM((256, 1152), BF16),
            pltpu.VMEM((8, 3, 80, 256), BF16),
            pltpu.VMEM((8, 3, 80, 256), BF16),
            pltpu.VMEM((2048, 80), BF16),
            pltpu.VMEM((80, 2048), BF16),
            pltpu.VMEM((8, 80, 256), BF16),
            pltpu.VMEM((8, 80, 256), BF16),
            pltpu.VMEM((8, 32, 640), BF16),
            pltpu.VMEM((8, 32, 640), BF16),
            pltpu.SemaphoreType.DMA((8,)),
            pltpu.SemaphoreType.DMA((16,)),
            pltpu.SemaphoreType.DMA((3,)),
            pltpu.SemaphoreType.DMA((3,)),
            pltpu.SemaphoreType.DMA((2, 8)),
            pltpu.SemaphoreType.DMA((2, 8)),
            pltpu.SemaphoreType.DMA((3, 8)),
            pltpu.SemaphoreType.DMA((3, 8)),
            pltpu.SemaphoreType.DMA((7,)),
            pltpu.SemaphoreType.DMA((7,)),
            pltpu.SemaphoreType.DMA((42,)),
            pltpu.SemaphoreType.DMA((42,)),
        ],
        compiler_params=pltpu.CompilerParams(
            collective_id=0, has_side_effects=True, vmem_limit_bytes=60 * 1024 * 1024
        ),
        name="decoder_block",
    )(
        jnp.transpose(features, (0, 1, 3, 2)),
        jnp.transpose(head_weight, (0, 2, 1)),
        norm_gain,
        head_bias,
        frame_order,
        combine_matrix(),
        column_matrix(),
        order_matrix(),
        pos_embed,
        patch_weight,
        patch_bias,
        ln_gain,
        ln_bias,
        w_qkv.T,
        b_qkv,
        w_out,
        b_out,
    )


def solution(mesh):
    in_specs = (
        P("ta", "ha", None, None),
        P(),
        P(),
        P(),
        P(),
        P(),
        P(),
        P("ha", None),
        P(),
        P(),
        P(),
        P(),
        P(),
        P(),
    )
    out_specs = P("ta", "ha", None)
    return jax.shard_map(shards, mesh=mesh, in_specs=in_specs, out_specs=out_specs, check_vma=False)
```

```python
import functools

import jax
import jax.numpy as jnp
import numpy as np
from jax import lax
from jax.experimental import pallas as pl
from jax.experimental.pallas import tpu as pltpu
from jax.sharding import PartitionSpec as P

HEADS = 8
HD = 72
MESH = pl.DeviceIdType.MESH
F32 = jnp.float32
BF16 = jnp.bfloat16

P_ORDER = [0, 13] + list(range(1, 13))


def shifted(g, j):
    return 1 if (g == 0 and j == 0) or (g == 1 and j == 2) else 0


def combine_matrix():
    m = np.zeros((192, 224), np.float32)
    for g in range(2):
        for j in range(3):
            base = shifted(g, j) * 96 + g * 48
            for c in range(3):
                for at, p in enumerate(P_ORDER):
                    r, h = divmod(p, 2)
                    for i in range(3):
                        source = r + (h + i - 1) // 2
                        if 0 <= source < 7:
                            m[base + at * 3 + c, source * 32 + 9 * i + 3 * j + c] = 1
    return m.astype(jnp.bfloat16)


def edge_matrix():
    m = np.zeros((64, 64), np.float32)
    for g in range(2):
        for j in range(3):
            base = shifted(g, j) * 32 + g * 16
            for c in range(3):
                m[base + c, 32 + 3 * j + c] = 1
                m[base + 8 + 3 + c, 18 + 3 * j + c] = 1
    return m.astype(jnp.bfloat16)


def column_matrix():
    m = np.zeros((224, 256), np.float32)
    for x in range(7):
        for token in range(32):
            m[x * 32 + token, 7 * token + x] = 1
    return m.astype(jnp.bfloat16)


def order_matrix():
    m = np.zeros((640, 588), np.float32)
    for q in range(14):
        for at, p in enumerate(P_ORDER):
            for c in range(3):
                m[q * 42 + at * 3 + c, 3 * (14 * p + q) + c] = 1
    return m.astype(jnp.bfloat16)


def remote(src, dst, send, recv, peer):
    return pltpu.make_async_remote_copy(
        src_ref=src, dst_ref=dst, send_sem=send, recv_sem=recv, device_id=peer, device_id_type=MESH
    )


def kernel(
    x_hbm,
    taps_hbm,
    gain_hbm,
    bias_hbm,
    order_hbm,
    combine_hbm,
    edge_hbm,
    column_hbm,
    perm_hbm,
    pos_hbm,
    pw_hbm,
    pb_hbm,
    lng_hbm,
    lnb_hbm,
    wqkv_hbm,
    bqkv_hbm,
    wout_hbm,
    bout_hbm,
    out_ref,
    x_ref,
    taps_ref,
    gain_ref,
    bias_ref,
    order_ref,
    combine_ref,
    edge_ref,
    column_ref,
    perm_ref,
    pos_ref,
    pw_ref,
    pb_ref,
    lng_ref,
    lnb_ref,
    wqkv_ref,
    bqkv_ref,
    wout_ref,
    bout_ref,
    w_ref,
    acc,
    vs,
    edn,
    eup,
    vin,
    edn_c,
    eup_c,
    edn_in,
    eup_in,
    pw_all,
    gathered,
    pos_in,
    own_ref,
    x_in,
    resid,
    normed,
    q_out,
    q_in,
    k_all,
    v_all,
    c_out,
    c_in,
    z_out,
    z_in,
    x_sem,
    load_sem,
    near_send,
    near_recv,
    ring_send,
    ring_recv,
    pos_send,
    pos_recv,
    send_sem,
    recv_sem,
):
    s = lax.axis_index("ha")
    t = lax.axis_index("ta")
    z = s // 8
    q = s % 8
    below = lax.rem(s + 1, 64)
    above = lax.rem(s + 63, 64)
    after = lax.rem(t + 1, 4)
    prior = lax.rem(t + 3, 4)

    names = [
        "taps",
        "gain",
        "bias",
        "order",
        "combine",
        "edge",
        "column",
        "perm",
        "pos",
        "pw",
        "pb",
        "lng",
        "lnb",
        "wqkv",
        "bqkv",
        "wout",
        "bout",
    ]
    sources = [
        (taps_hbm, taps_ref),
        (gain_hbm, gain_ref),
        (bias_hbm, bias_ref),
        (order_hbm, order_ref),
        (combine_hbm, combine_ref),
        (edge_hbm, edge_ref),
        (column_hbm, column_ref),
        (perm_hbm, perm_ref),
        (pos_hbm, pos_ref),
        (pw_hbm, pw_ref),
        (pb_hbm, pb_ref),
        (lng_hbm, lng_ref),
        (lnb_hbm, lnb_ref),
        (wqkv_hbm, wqkv_ref),
        (bqkv_hbm, bqkv_ref),
        (wout_hbm, wout_ref),
        (bout_hbm, bout_ref),
    ]
    loads = {
        name: pltpu.make_async_copy(source, target, load_sem.at[at])
        for at, (name, (source, target)) in enumerate(zip(names, sources))
    }

    def ready(*wanted):
        for name in wanted:
            loads.pop(name).wait()

    loads["taps"].start()
    loads["gain"].start()
    rows_in = [
        pltpu.make_async_copy(x_hbm.at[:, r], x_ref.at[:, r], x_sem.at[at])
        for at, r in ((8, 0), (9, 6))
    ]

    def inner(f):
        return pltpu.make_async_copy(
            x_hbm.at[f, pl.ds(1, 5)], x_ref.at[f, pl.ds(1, 5)], x_sem.at[f]
        )

    for copy in rows_in:
        copy.start()
    loads["edge"].start()
    for f in [6, 7, 0, 1, 2, 3, 4, 5]:
        inner(f).start()
    for name in names[2:]:
        if name != "edge":
            loads[name].start()

    planes = [lax.rem(z + d, 8) for d in range(1, 8)]
    heads = [lax.rem(q + d, 8) for d in range(1, 8)]
    ring = [{"ha": s, "ta": lax.rem(t + d, 4)} for d in range(1, 4)]
    column = [{"ha": plane * 8 + q, "ta": t} for plane in planes]
    cluster = [{"ha": z * 8 + head, "ta": t} for head in heads]
    near = [
        {"ha": below, "ta": t},
        {"ha": above, "ta": t},
        {"ha": below, "ta": after},
        {"ha": above, "ta": after},
        {"ha": below, "ta": prior},
        {"ha": above, "ta": prior},
    ]

    peers = ring + column + cluster + near
    barrier = pltpu.get_barrier_semaphore()
    for peer in peers:
        pl.semaphore_signal(barrier, inc=1, device_id=peer, device_id_type=MESH)

    w_ref[...] = jnp.zeros_like(w_ref)
    ready("taps", "gain")
    for tap in range(3):
        w_ref[tap, 0:27, :] = taps_ref[tap].astype(F32)
    acc[...] = jnp.zeros_like(acc)
    gain = jnp.transpose(jnp.broadcast_to(0.5 * gain_ref[...].reshape(1, 192), (8, 192)))[:, 0:1]
    weight = w_ref[...].reshape(96, 192).astype(BF16)

    def convolve(f, which):
        for r in which:
            x = x_ref[f, r].astype(F32)
            factor = lax.rsqrt(jnp.sum(x * x, axis=0, keepdims=True) * (1.0 / 192.0) + 1e-06)
            u = x * factor * gain
            a = (u + u * jnp.tanh(u)).astype(BF16)
            res = jnp.dot(weight, a, preferred_element_type=F32)
            rows = pl.ds(r * 32, 32)
            acc[f, rows, 0:224] += res[64:96]
            acc[f + 1, rows, 0:224] += res[32:64]
            acc[f + 2, rows, 0:224] += res[0:32]

    def combine(f):
        total = acc[f]
        high = total.astype(BF16)
        low = (total - high.astype(F32)).astype(BF16)
        m = combine_ref[...]
        y = jnp.dot(m, high, preferred_element_type=F32) + jnp.dot(
            m, low, preferred_element_type=F32
        )
        for g in range(2):
            moved = pltpu.roll(y[96 + 48 * g : 144 + 48 * g], 1 if g == 0 else 255, 1)
            vs[f, g] = y[48 * g : 48 * g + 48] + moved

    def edge_rows(f, carry):
        total = jnp.concatenate([acc[f, 0:32], acc[f, 192:224]], axis=0)
        high = total.astype(BF16)
        low = (total - high.astype(F32)).astype(BF16)
        m = edge_ref[...]
        y = jnp.dot(m, high, preferred_element_type=F32) + jnp.dot(
            m, low, preferred_element_type=F32
        )
        for g in range(2):
            moved = pltpu.roll(y[32 + 16 * g : 48 + 16 * g], 1 if g == 0 else 255, 1)
            v = y[16 * g : 16 * g + 16] + moved
            edn[f, g] = v[0:8]
            eup[f, g] = v[8:16]
        return carry

    def outer_rows(f, carry):
        convolve(f, (0, 6))
        return carry

    def inner_rows(f, carry):
        inner(f).wait()
        convolve(f, (1, 2, 3, 4, 5))
        return carry

    colour = lax.rem(lax.broadcasted_iota(jnp.int32, (48, 256), 0), 3)
    from_above = s > 0
    from_below = s < 63
    from_prior = t > 0

    def spread(f):
        slot = t * 8 + f
        return [
            remote(
                gathered.at[slot],
                gathered.at[slot],
                ring_send.at[d, f],
                ring_recv.at[d, f],
                ring[d],
            )
            for d in range(3)
        ]

    def finish(f):
        bias = jnp.where(colour == 0, bias_ref[0], jnp.where(colour == 1, bias_ref[1], bias_ref[2]))
        parts = []
        for g in range(2):
            edge = jnp.where(from_above, edn_in[f, g], 0.0) + jnp.where(
                from_below, eup_in[f, g], 0.0
            )
            v = vs[f, g] + bias
            parts += [v[0:8] + edge, v[8:48]]
        v = jnp.concatenate(parts, axis=0).astype(BF16)
        cols = lax.dot_general(
            column_ref[...], v, (((1,), (1,)), ((), ())), preferred_element_type=F32
        )
        pieces = [
            cols[x * 32 : (x + 1) * 32, g * 48 : g * 48 + 42] for x in range(7) for g in range(2)
        ]
        pieces.append(jnp.zeros((32, 52), F32))
        gathered[t * 8 + f] = jnp.concatenate(pieces, axis=1).astype(BF16)
        for copy in spread(f):
            copy.start()

    right = {"ha": lax.rem(z + 1, 8) * 8 + q, "ta": t}
    left = {"ha": lax.rem(z + 7, 8) * 8 + q, "ta": t}

    def relay(k, way):
        slot = lax.rem(z + 8 - k, 8) if way == 0 else lax.rem(z + k, 8)
        return remote(
            pos_in.at[slot],
            pos_in.at[slot],
            pos_send.at[way, k],
            pos_recv.at[way, k],
            right if way == 0 else left,
        )

    def relay_start(k):
        for way in (0, 1) if k < 3 else (0,):
            relay(k, way).start()

    def relay_wait(k):
        for way in (0, 1) if k < 3 else (0,):
            relay(k, way).wait()

    for copy in rows_in:
        copy.wait()
    lax.fori_loop(0, 8, outer_rows, 0)
    ready("edge", "pos")
    lax.fori_loop(0, 10, edge_rows, 0)
    pos_in[z] = pos_ref[...]
    tail = pl.ds(8, 2)
    body = pl.ds(0, 8)
    halo = [
        remote(edn.at[body], edn_in, near_send.at[0], near_recv.at[0], near[0]),
        remote(eup.at[body], eup_in, near_send.at[1], near_recv.at[1], near[1]),
        remote(edn.at[tail], edn_c, near_send.at[2], near_recv.at[2], near[2]),
        remote(eup.at[tail], eup_c, near_send.at[3], near_recv.at[3], near[3]),
        remote(vs.at[tail], vin, near_send.at[4], near_recv.at[4], {"ha": s, "ta": after}),
    ]
    pl.semaphore_wait(barrier, len(peers))
    for copy in halo[:4]:
        copy.start()
    relay_start(0)
    lax.fori_loop(6, 8, inner_rows, 0)
    ready("combine")
    for f in (8, 9):
        combine(f)
    halo[4].start()
    relay_wait(0)
    relay_start(1)
    lax.fori_loop(0, 2, inner_rows, 0)
    ready("bias", "column")
    relay_wait(1)
    relay_start(2)
    lax.fori_loop(2, 3, inner_rows, 0)
    for f in range(3):
        combine(f)
    for copy in halo:
        copy.wait()
    for first in range(2):
        for g in range(2):
            extra = jnp.where(from_prior, vin[first, g], 0.0)
            corner = jnp.where(from_prior & from_above, edn_c[first, g], 0.0) + jnp.where(
                from_prior & from_below, eup_c[first, g], 0.0
            )
            vs[first, g] += extra
            vs[first, g, 0:8] += corner

    def finish_one(f, carry):
        finish(f)
        return carry

    def early(f, carry):
        inner_rows(f, carry)
        combine(f)
        finish(f)
        return carry

    lax.fori_loop(0, 3, finish_one, 0)
    relay_wait(2)
    relay_start(3)
    lax.fori_loop(3, 6, early, 0)
    for f in (6, 7):
        combine(f)
    lax.fori_loop(6, 8, finish_one, 0)
    ready("perm", "pw", "order")
    pw_all[...] = jnp.dot(perm_ref[...], pw_ref[...], preferred_element_type=F32).astype(BF16)
    for f in range(8):
        for copy in spread(f):
            copy.wait()
    for j in range(8):
        own_ref[j] = gathered[order_ref[t * 8 + j]]

    frames = []
    for d in range(7):
        copy = remote(
            own_ref.at[planes[d]], x_in.at[z], send_sem.at[d], recv_sem.at[d], column[d]
        )
        copy.start()
        frames.append(copy)
    x_in[z] = own_ref[z]

    row = lax.broadcasted_iota(jnp.int32, (80, 256), 0)
    for h in range(8):
        q_out[h, 0] = jnp.zeros((80, 256), BF16)
        q_out[h, 1] = jnp.zeros((80, 256), BF16)
        q_out[h, 2] = jnp.where(row == HD, 1.0, 0.0).astype(BF16)
    z_out[...] = jnp.zeros_like(z_out)

    def embed(tokens, positions):
        value = jnp.dot(
            tokens.reshape(256, 640), pw_all[...], preferred_element_type=F32
        ).reshape(8, 32, 1152)
        return (value + pb_ref[...].reshape(1, 1, 1152) + positions.astype(F32)).astype(BF16)

    ready("pb")
    resid[...] = embed(own_ref[...], pos_ref[...].reshape(1, 32, 1152)).reshape(256, 1152)
    ready("lng", "lnb", "bqkv", "wqkv")
    bias = jnp.transpose(jnp.broadcast_to(bqkv_ref[...].reshape(1, 1728), (8, 1728)))[:, 0:1]
    for copy in frames:
        copy.wait()
    relay_wait(3)
    value = embed(x_in[...], pos_in[...]).reshape(256, 1152).astype(F32)
    centre = jnp.mean(value, axis=-1, keepdims=True)
    value = value - centre
    spread = jnp.mean(value * value, axis=-1, keepdims=True)
    normed[...] = (value * lax.rsqrt(spread + 1e-06) * lng_ref[...].reshape(1, 1152) + lnb_ref[...].reshape(1, 1152)).astype(BF16)

    pairs = {}
    for kind in (1, 2, 0):
        rows = slice(kind * 576, kind * 576 + 576)
        made = (
            lax.dot_general(
                wqkv_ref[rows, :], normed[...], (((1,), (1,)), ((), ())), preferred_element_type=F32
            )
            + bias[rows]
        ).astype(F32)
        for h in range(8):
            q_out[h, kind, 0:HD] = made[h * HD : (h + 1) * HD].astype(BF16)
        for d in range(7):
            at = 7 + kind * 7 + d
            copy = remote(
                q_out.at[heads[d], kind],
                q_in.at[q, kind],
                send_sem.at[at],
                recv_sem.at[at],
                cluster[d],
            )
            copy.start()
            pairs[kind, d] = copy
        q_in[q, kind] = q_out[q, kind]

    for d in range(7):
        pairs[1, d].wait()
    for p in range(8):
        k_all[p * 256 : (p + 1) * 256, :] = jnp.transpose(q_in[p, 1].astype(F32)).astype(BF16)
    for d in range(7):
        pairs[2, d].wait()
    for p in range(8):
        v_all[:, p * 256 : (p + 1) * 256] = q_in[p, 2]
    for d in range(7):
        pairs[0, d].wait()

    rate = HD ** (-0.5) * 1.4426950408889634

    def attend(i, carry):
        p = lax.rem(q + 1 + i, 8)
        scores = jnp.dot(k_all[...], q_in[p, 0], preferred_element_type=F32)
        highest = jnp.max(scores, axis=0, keepdims=True)
        weights = jnp.exp2((scores - highest) * rate).astype(BF16)
        mixed = jnp.dot(v_all[...], weights, preferred_element_type=F32)
        c_out[p] = (mixed / mixed[HD : HD + 1]).astype(BF16)

        @pl.when(i < 7)
        def _():
            remote(
                c_out.at[p],
                c_in.at[q],
                send_sem.at[28 + i],
                recv_sem.at[28 + i],
                {"ha": z * 8 + p, "ta": t},
            ).start()

        return carry

    lax.fori_loop(0, 8, attend, 0)
    c_in[q] = c_out[q]
    for d in range(7):
        remote(
            c_out.at[heads[d]], c_in.at[q], send_sem.at[28 + d], recv_sem.at[28 + d], cluster[d]
        ).wait()
    sides = jnp.concatenate([c_in[h, 0:HD].astype(F32) for h in range(8)], axis=0)
    z_out[:, :, 0:576] = jnp.transpose(sides).astype(BF16).reshape(8, 32, 576)
    backs = []
    for d in range(7):
        copy = remote(
            z_out.at[planes[d]], z_in.at[z], send_sem.at[35 + d], recv_sem.at[35 + d], column[d]
        )
        copy.start()
        backs.append(copy)
    z_in[z] = z_out[z]
    ready("wout", "bout")
    for copy in backs:
        copy.wait()
    result = jnp.dot(
        z_in[...].reshape(256, 640)[:, :576], wout_ref[...], preferred_element_type=F32
    )
    result = result + bout_ref[...].reshape(1, 1152) + resid[...].astype(F32)
    out_ref[...] = result.astype(BF16).reshape(8, 32, 1152)


def shards(
    features,
    norm_gain,
    head_weight,
    head_bias,
    frame_order,
    patch_weight,
    patch_bias,
    pos_embed,
    ln_gain,
    ln_bias,
    w_qkv,
    b_qkv,
    w_out,
    b_out,
):
    hbm = pl.BlockSpec(memory_space=pl.ANY)
    vmem = pl.BlockSpec(memory_space=pltpu.VMEM)
    return pl.pallas_call(
        kernel,
        out_shape=jax.ShapeDtypeStruct((8, 32, 1152), BF16),
        in_specs=[hbm] * 18,
        out_specs=vmem,
        scratch_shapes=[
            pltpu.VMEM((8, 7, 192, 224), BF16),
            pltpu.VMEM((3, 27, 192), BF16),
            pltpu.VMEM((192,), F32),
            pltpu.SMEM((3,), F32),
            pltpu.SMEM((32,), jnp.int32),
            pltpu.VMEM((192, 224), BF16),
            pltpu.VMEM((64, 64), BF16),
            pltpu.VMEM((224, 256), BF16),
            pltpu.VMEM((640, 588), BF16),
            pltpu.VMEM((32, 1152), BF16),
            pltpu.VMEM((588, 1152), BF16),
            pltpu.VMEM((1152,), F32),
            pltpu.VMEM((1152,), F32),
            pltpu.VMEM((1152,), F32),
            pltpu.VMEM((1728, 1152), BF16),
            pltpu.VMEM((1728,), F32),
            pltpu.VMEM((576, 1152), BF16),
            pltpu.VMEM((1152,), F32),
            pltpu.VMEM((3, 32, 192), F32),
            pltpu.VMEM((10, 224, 256), F32),
            pltpu.VMEM((10, 2, 48, 256), F32),
            pltpu.VMEM((10, 2, 8, 256), F32),
            pltpu.VMEM((10, 2, 8, 256), F32),
            pltpu.VMEM((2, 2, 48, 256), F32),
            pltpu.VMEM((2, 2, 8, 256), F32),
            pltpu.VMEM((2, 2, 8, 256), F32),
            pltpu.VMEM((8, 2, 8, 256), F32),
            pltpu.VMEM((8, 2, 8, 256), F32),
            pltpu.VMEM((640, 1152), BF16),
            pltpu.VMEM((32, 32, 640), BF16),
            pltpu.VMEM((8, 32, 1152), BF16),
            pltpu.VMEM((8, 32, 640), BF16),
            pltpu.VMEM((8, 32, 640), BF16),
            pltpu.VMEM((256, 1152), BF16),
            pltpu.VMEM((256, 1152), BF16),
            pltpu.VMEM((8, 3, 80, 256), BF16),
            pltpu.VMEM((8, 3, 80, 256), BF16),
            pltpu.VMEM((2048, 80), BF16),
            pltpu.VMEM((80, 2048), BF16),
            pltpu.VMEM((8, 80, 256), BF16),
            pltpu.VMEM((8, 80, 256), BF16),
            pltpu.VMEM((8, 32, 640), BF16),
            pltpu.VMEM((8, 32, 640), BF16),
            pltpu.SemaphoreType.DMA((10,)),
            pltpu.SemaphoreType.DMA((17,)),
            pltpu.SemaphoreType.DMA((5,)),
            pltpu.SemaphoreType.DMA((5,)),
            pltpu.SemaphoreType.DMA((3, 8)),
            pltpu.SemaphoreType.DMA((3, 8)),
            pltpu.SemaphoreType.DMA((2, 4)),
            pltpu.SemaphoreType.DMA((2, 4)),
            pltpu.SemaphoreType.DMA((42,)),
            pltpu.SemaphoreType.DMA((42,)),
        ],
        compiler_params=pltpu.CompilerParams(
            collective_id=0, has_side_effects=True, vmem_limit_bytes=60 * 1024 * 1024
        ),
        name="decoder_block",
    )(
        jnp.transpose(features, (0, 1, 3, 2)),
        jnp.transpose(head_weight, (0, 2, 1)),
        norm_gain,
        head_bias,
        frame_order,
        combine_matrix(),
        edge_matrix(),
        column_matrix(),
        order_matrix(),
        pos_embed,
        patch_weight,
        patch_bias,
        ln_gain,
        ln_bias,
        w_qkv.T,
        b_qkv,
        w_out,
        b_out,
    )


def solution(mesh):
    in_specs = (
        P("ta", "ha", None, None),
        P(),
        P(),
        P(),
        P(),
        P(),
        P(),
        P("ha", None),
        P(),
        P(),
        P(),
        P(),
        P(),
        P(),
    )
    out_specs = P("ta", "ha", None)
    return jax.shard_map(shards, mesh=mesh, in_specs=in_specs, out_specs=out_specs, check_vma=False)
```

```python
import functools

import jax
import jax.numpy as jnp
import numpy as np
from jax import lax
from jax.experimental import pallas as pl
from jax.experimental.pallas import tpu as pltpu
from jax.sharding import PartitionSpec as P

HEADS = 8
HD = 72
MESH = pl.DeviceIdType.MESH
F32 = jnp.float32
BF16 = jnp.bfloat16

P_ORDER = [0, 13] + list(range(1, 13))


def shifted(g, j):
    return 1 if (g == 0 and j == 0) or (g == 1 and j == 2) else 0


def combine_matrix():
    m = np.zeros((192, 224), np.float32)
    for g in range(2):
        for j in range(3):
            base = shifted(g, j) * 96 + g * 48
            for c in range(3):
                for at, p in enumerate(P_ORDER):
                    r, h = divmod(p, 2)
                    for i in range(3):
                        source = r + (h + i - 1) // 2
                        if 0 <= source < 7:
                            m[base + at * 3 + c, source * 32 + 9 * i + 3 * j + c] = 1
    return m.astype(jnp.bfloat16)


def edge_matrix():
    m = np.zeros((64, 64), np.float32)
    for g in range(2):
        for j in range(3):
            base = shifted(g, j) * 32 + g * 16
            for c in range(3):
                m[base + c, 32 + 3 * j + c] = 1
                m[base + 8 + 3 + c, 18 + 3 * j + c] = 1
    return m.astype(jnp.bfloat16)


def column_matrix():
    m = np.zeros((224, 256), np.float32)
    for x in range(7):
        for token in range(32):
            m[x * 32 + token, 7 * token + x] = 1
    return m.astype(jnp.bfloat16)


def order_matrix():
    m = np.zeros((640, 588), np.float32)
    for q in range(14):
        for at, p in enumerate(P_ORDER):
            for c in range(3):
                m[q * 42 + at * 3 + c, 3 * (14 * p + q) + c] = 1
    return m.astype(jnp.bfloat16)


def remote(src, dst, send, recv, peer):
    return pltpu.make_async_remote_copy(
        src_ref=src, dst_ref=dst, send_sem=send, recv_sem=recv, device_id=peer, device_id_type=MESH
    )


def kernel(
    x_hbm,
    taps_hbm,
    gain_hbm,
    bias_hbm,
    order_hbm,
    combine_hbm,
    edge_hbm,
    column_hbm,
    perm_hbm,
    pos_hbm,
    pw_hbm,
    pb_hbm,
    lng_hbm,
    lnb_hbm,
    wqkv_hbm,
    bqkv_hbm,
    wout_hbm,
    bout_hbm,
    out_ref,
    x_ref,
    taps_ref,
    gain_ref,
    bias_ref,
    order_ref,
    combine_ref,
    edge_ref,
    column_ref,
    perm_ref,
    pos_ref,
    pw_ref,
    pb_ref,
    lng_ref,
    lnb_ref,
    wqkv_ref,
    bqkv_ref,
    wout_ref,
    bout_ref,
    w_ref,
    acc,
    vs,
    edn,
    eup,
    vin,
    edn_c,
    eup_c,
    edn_in,
    eup_in,
    pw_all,
    gathered_a,
    gathered_b,
    pos_in,
    own_ref,
    x_in,
    resid,
    normed,
    q_out,
    q_in,
    k_all,
    v_all,
    c_out,
    c_in,
    z_out,
    z_in,
    x_sem,
    load_sem,
    near_send,
    near_recv,
    ring_send,
    ring_recv,
    pos_send,
    pos_recv,
    send_sem,
    recv_sem,
):
    s = lax.axis_index("ha")
    t = lax.axis_index("ta")
    z = s // 8
    q = s % 8
    below = lax.rem(s + 1, 64)
    above = lax.rem(s + 63, 64)
    after = lax.rem(t + 1, 4)
    prior = lax.rem(t + 3, 4)

    names = [
        "taps",
        "gain",
        "bias",
        "order",
        "combine",
        "edge",
        "column",
        "perm",
        "pos",
        "pw",
        "pb",
        "lng",
        "lnb",
        "wqkv",
        "bqkv",
        "wout",
        "bout",
    ]
    sources = [
        (taps_hbm, taps_ref),
        (gain_hbm, gain_ref),
        (bias_hbm, bias_ref),
        (order_hbm, order_ref),
        (combine_hbm, combine_ref),
        (edge_hbm, edge_ref),
        (column_hbm, column_ref),
        (perm_hbm, perm_ref),
        (pos_hbm, pos_ref),
        (pw_hbm, pw_ref),
        (pb_hbm, pb_ref),
        (lng_hbm, lng_ref),
        (lnb_hbm, lnb_ref),
        (wqkv_hbm, wqkv_ref),
        (bqkv_hbm, bqkv_ref),
        (wout_hbm, wout_ref),
        (bout_hbm, bout_ref),
    ]
    loads = {
        name: pltpu.make_async_copy(source, target, load_sem.at[at])
        for at, (name, (source, target)) in enumerate(zip(names, sources))
    }

    def ready(*wanted):
        for name in wanted:
            loads.pop(name).wait()

    loads["taps"].start()
    loads["gain"].start()
    rows_in = [
        pltpu.make_async_copy(x_hbm.at[:, r], x_ref.at[:, r], x_sem.at[at])
        for at, r in ((8, 0), (9, 6))
    ]

    def inner(f):
        return pltpu.make_async_copy(
            x_hbm.at[f, pl.ds(1, 5)], x_ref.at[f, pl.ds(1, 5)], x_sem.at[f]
        )

    for copy in rows_in:
        copy.start()
    loads["edge"].start()
    for f in [6, 7, 0, 1, 2, 3, 4, 5]:
        inner(f).start()
    for name in names[2:]:
        if name != "edge":
            loads[name].start()

    planes = [lax.rem(z + d, 8) for d in range(1, 8)]
    heads = [lax.rem(q + d, 8) for d in range(1, 8)]
    ring = [{"ha": s, "ta": lax.rem(t + d, 4)} for d in range(1, 4)]
    column = [{"ha": plane * 8 + q, "ta": t} for plane in planes]
    cluster = [{"ha": z * 8 + head, "ta": t} for head in heads]
    near = [
        {"ha": below, "ta": t},
        {"ha": above, "ta": t},
        {"ha": below, "ta": after},
        {"ha": above, "ta": after},
        {"ha": below, "ta": prior},
        {"ha": above, "ta": prior},
    ]

    peers = ring + column + cluster + near
    barrier = pltpu.get_barrier_semaphore()
    for peer in peers:
        pl.semaphore_signal(barrier, inc=1, device_id=peer, device_id_type=MESH)

    w_ref[...] = jnp.zeros_like(w_ref)
    ready("taps", "gain")
    for tap in range(3):
        w_ref[tap, 0:27, :] = taps_ref[tap].astype(F32)
    acc[...] = jnp.zeros_like(acc)
    gain = jnp.transpose(jnp.broadcast_to(0.5 * gain_ref[...].reshape(1, 192), (8, 192)))[:, 0:1]
    weight = w_ref[...].reshape(96, 192).astype(BF16)

    def convolve(f, which):
        for r in which:
            x = x_ref[f, r].astype(F32)
            factor = lax.rsqrt(jnp.sum(x * x, axis=0, keepdims=True) * (1.0 / 192.0) + 1e-06)
            u = x * factor * gain
            a = (u + u * jnp.tanh(u)).astype(BF16)
            res = jnp.dot(weight, a, preferred_element_type=F32)
            rows = pl.ds(r * 32, 32)
            acc[f, rows, 0:224] += res[64:96]
            acc[f + 1, rows, 0:224] += res[32:64]
            acc[f + 2, rows, 0:224] += res[0:32]

    def combine(f):
        total = acc[f]
        high = total.astype(BF16)
        low = (total - high.astype(F32)).astype(BF16)
        m = combine_ref[...]
        y = jnp.dot(m, high, preferred_element_type=F32) + jnp.dot(
            m, low, preferred_element_type=F32
        )
        for g in range(2):
            moved = pltpu.roll(y[96 + 48 * g : 144 + 48 * g], 1 if g == 0 else 255, 1)
            vs[f, g] = y[48 * g : 48 * g + 48] + moved

    def edge_rows(f, carry):
        total = jnp.concatenate([acc[f, 0:32], acc[f, 192:224]], axis=0)
        high = total.astype(BF16)
        low = (total - high.astype(F32)).astype(BF16)
        m = edge_ref[...]
        y = jnp.dot(m, high, preferred_element_type=F32) + jnp.dot(
            m, low, preferred_element_type=F32
        )
        for g in range(2):
            moved = pltpu.roll(y[32 + 16 * g : 48 + 16 * g], 1 if g == 0 else 255, 1)
            v = y[16 * g : 16 * g + 16] + moved
            edn[f, g] = v[0:8]
            eup[f, g] = v[8:16]
        return carry

    def outer_rows(f, carry):
        convolve(f, (0, 6))
        return carry

    def inner_rows(f, carry):
        inner(f).wait()
        convolve(f, (1, 2, 3, 4, 5))
        return carry

    colour = lax.rem(lax.broadcasted_iota(jnp.int32, (48, 256), 0), 3)
    from_above = s > 0
    from_below = s < 63
    from_prior = t > 0

    gathered = (gathered_a, gathered_b)

    def spread(half, f):
        slot = t * 8 + f
        return [
            remote(
                gathered[half].at[slot],
                gathered[half].at[slot],
                ring_send.at[half, d, f],
                ring_recv.at[half, d, f],
                ring[d],
            )
            for d in range(3)
        ]

    def finish(f):
        bias = jnp.where(colour == 0, bias_ref[0], jnp.where(colour == 1, bias_ref[1], bias_ref[2]))
        parts = []
        for g in range(2):
            edge = jnp.where(from_above, edn_in[f, g], 0.0) + jnp.where(
                from_below, eup_in[f, g], 0.0
            )
            v = vs[f, g] + bias
            parts += [v[0:8] + edge, v[8:48]]
        v = jnp.concatenate(parts, axis=0).astype(BF16)
        cols = lax.dot_general(
            column_ref[...], v, (((1,), (1,)), ((), ())), preferred_element_type=F32
        )
        pieces = [
            cols[x * 32 : (x + 1) * 32, g * 48 : g * 48 + 42] for x in range(7) for g in range(2)
        ]
        pieces.append(jnp.zeros((32, 52), F32))
        tokens = jnp.concatenate(pieces, axis=1).astype(BF16)
        for half in range(2):
            gathered[half][t * 8 + f] = tokens[16 * half : 16 * half + 16]
        for copy in spread(0, f):
            copy.start()

    right = {"ha": lax.rem(z + 1, 8) * 8 + q, "ta": t}
    left = {"ha": lax.rem(z + 7, 8) * 8 + q, "ta": t}

    def relay(k, way):
        slot = lax.rem(z + 8 - k, 8) if way == 0 else lax.rem(z + k, 8)
        return remote(
            pos_in.at[slot],
            pos_in.at[slot],
            pos_send.at[way, k],
            pos_recv.at[way, k],
            right if way == 0 else left,
        )

    def relay_start(k):
        for way in (0, 1) if k < 3 else (0,):
            relay(k, way).start()

    def relay_wait(k):
        for way in (0, 1) if k < 3 else (0,):
            relay(k, way).wait()

    for copy in rows_in:
        copy.wait()
    lax.fori_loop(0, 8, outer_rows, 0)
    ready("edge", "pos")
    lax.fori_loop(0, 10, edge_rows, 0)
    pos_in[z] = pos_ref[...]
    tail = pl.ds(8, 2)
    body = pl.ds(0, 8)
    halo = [
        remote(edn.at[body], edn_in, near_send.at[0], near_recv.at[0], near[0]),
        remote(eup.at[body], eup_in, near_send.at[1], near_recv.at[1], near[1]),
        remote(edn.at[tail], edn_c, near_send.at[2], near_recv.at[2], near[2]),
        remote(eup.at[tail], eup_c, near_send.at[3], near_recv.at[3], near[3]),
        remote(vs.at[tail], vin, near_send.at[4], near_recv.at[4], {"ha": s, "ta": after}),
    ]
    pl.semaphore_wait(barrier, len(peers))
    for copy in halo[:4]:
        copy.start()
    relay_start(0)
    lax.fori_loop(6, 8, inner_rows, 0)
    ready("combine")
    for f in (8, 9):
        combine(f)
    halo[4].start()
    lax.fori_loop(0, 2, inner_rows, 0)
    ready("bias", "column")
    lax.fori_loop(2, 3, inner_rows, 0)
    for f in range(3):
        combine(f)
    for copy in halo:
        copy.wait()
    for first in range(2):
        for g in range(2):
            extra = jnp.where(from_prior, vin[first, g], 0.0)
            corner = jnp.where(from_prior & from_above, edn_c[first, g], 0.0) + jnp.where(
                from_prior & from_below, eup_c[first, g], 0.0
            )
            vs[first, g] += extra
            vs[first, g, 0:8] += corner

    def finish_one(f, carry):
        finish(f)
        return carry

    def early(f, carry):
        inner_rows(f, carry)
        combine(f)
        finish(f)
        return carry

    relay_wait(0)
    relay_start(1)
    lax.fori_loop(0, 3, finish_one, 0)
    relay_wait(1)
    relay_start(2)
    lax.fori_loop(3, 6, early, 0)
    relay_wait(2)
    relay_start(3)
    for f in (6, 7):
        combine(f)
    lax.fori_loop(6, 8, finish_one, 0)
    for f in range(8):
        for copy in spread(1, f):
            copy.start()
    ready("perm", "pw", "order")
    pw_all[...] = jnp.dot(perm_ref[...], pw_ref[...], preferred_element_type=F32).astype(BF16)
    row = lax.broadcasted_iota(jnp.int32, (80, 128), 0)
    for half in range(2):
        for h in range(8):
            q_out[half, h, 0] = jnp.zeros((80, 128), BF16)
            q_out[half, h, 1] = jnp.zeros((80, 128), BF16)
            q_out[half, h, 2] = jnp.where(row == HD, 1.0, 0.0).astype(BF16)
    z_out[...] = jnp.zeros_like(z_out)
    ready("pb", "lng", "lnb", "bqkv", "wqkv")
    qkv_bias = jnp.transpose(jnp.broadcast_to(bqkv_ref[...].reshape(1, 1728), (8, 1728)))[:, 0:1]

    def frames(half):
        return [
            remote(
                own_ref.at[half, planes[d]],
                x_in.at[half, z],
                send_sem.at[7 * half + d],
                recv_sem.at[7 * half + d],
                column[d],
            )
            for d in range(7)
        ]

    def exchange(half):
        for f in range(8):
            for copy in spread(half, f):
                copy.wait()
        for j in range(8):
            own_ref[half, j] = gathered[half][order_ref[t * 8 + j]]
        for copy in frames(half):
            copy.start()
        x_in[half, z] = own_ref[half, z]

    def embed(tokens, positions):
        value = jnp.dot(
            tokens.reshape(128, 640), pw_all[...], preferred_element_type=F32
        ).reshape(8, 16, 1152)
        return (value + pb_ref[...].reshape(1, 1, 1152) + positions.astype(F32)).astype(BF16)

    def keep(half):
        here = slice(16 * half, 16 * half + 16)
        resid[:, here, :] = embed(own_ref[half], pos_ref[here, :].reshape(1, 16, 1152))

    def normalise(half):
        for copy in frames(half):
            copy.wait()
        here = slice(16 * half, 16 * half + 16)
        value = embed(x_in[half], pos_in[:, here, :]).reshape(128, 1152).astype(F32)
        centre = jnp.mean(value, axis=-1, keepdims=True)
        value = value - centre
        spread_out = jnp.mean(value * value, axis=-1, keepdims=True)
        normed[half] = (
            value * lax.rsqrt(spread_out + 1e-06) * lng_ref[...].reshape(1, 1152)
            + lnb_ref[...].reshape(1, 1152)
        ).astype(BF16)

    def pair(half, kind, d):
        at = 14 + half * 21 + kind * 7 + d
        return remote(
            q_out.at[half, heads[d], kind],
            q_in.at[half, q, kind],
            send_sem.at[at],
            recv_sem.at[at],
            cluster[d],
        )

    def project(half):
        for kind in (1, 0, 2):
            rows = slice(kind * 576, kind * 576 + 576)
            made = (
                lax.dot_general(
                    wqkv_ref[rows, :],
                    normed[half],
                    (((1,), (1,)), ((), ())),
                    preferred_element_type=F32,
                )
                + qkv_bias[rows]
            )
            for h in range(8):
                q_out[half, h, kind, 0:HD] = made[h * HD : (h + 1) * HD].astype(BF16)
            for d in range(7):
                pair(half, kind, d).start()
            q_in[half, q, kind] = q_out[half, q, kind]

    exchange(0)
    keep(0)
    relay_wait(3)
    normalise(0)
    exchange(1)
    project(0)
    keep(1)
    normalise(1)
    project(1)
    for half in range(2):
        for d in range(7):
            pair(half, 1, d).wait()
        for p in range(8):
            at = half * 1024 + p * 128
            k_all[at : at + 128, :] = jnp.transpose(q_in[half, p, 1].astype(F32)).astype(BF16)
        for d in range(7):
            pair(half, 0, d).wait()
    for half in range(2):
        for d in range(7):
            pair(half, 2, d).wait()
        for p in range(8):
            at = half * 1024 + p * 128
            v_all[:, at : at + 128] = q_in[half, p, 2]

    rate = HD ** (-0.5) * 1.4426950408889634

    def attend(i, carry):
        p = lax.rem(q + 1 + i, 8)
        asked = jnp.concatenate([q_in[0, p, 0], q_in[1, p, 0]], axis=1)
        scores = jnp.dot(k_all[...], asked, preferred_element_type=F32)
        highest = jnp.max(scores, axis=0, keepdims=True)
        weights = jnp.exp2((scores - highest) * rate).astype(BF16)
        mixed = jnp.dot(v_all[...], weights, preferred_element_type=F32)
        c_out[p] = (mixed / mixed[HD : HD + 1]).astype(BF16)

        @pl.when(i < 7)
        def _():
            remote(
                c_out.at[p],
                c_in.at[q],
                send_sem.at[56 + i],
                recv_sem.at[56 + i],
                {"ha": z * 8 + p, "ta": t},
            ).start()

        return carry

    lax.fori_loop(0, 8, attend, 0)
    c_in[q] = c_out[q]
    for d in range(7):
        remote(
            c_out.at[heads[d]], c_in.at[q], send_sem.at[56 + d], recv_sem.at[56 + d], cluster[d]
        ).wait()
    sides = jnp.concatenate([c_in[h, 0:HD].astype(F32) for h in range(8)], axis=0)
    merged = jnp.transpose(sides).astype(BF16).reshape(2, 8, 16, 576)
    for half in range(2):
        z_out[:, 16 * half : 16 * half + 16, 0:576] = merged[half]
    backs = []
    for d in range(7):
        copy = remote(
            z_out.at[planes[d]], z_in.at[z], send_sem.at[63 + d], recv_sem.at[63 + d], column[d]
        )
        copy.start()
        backs.append(copy)
    z_in[z] = z_out[z]
    ready("wout", "bout")
    for copy in backs:
        copy.wait()
    result = jnp.dot(
        z_in[...].reshape(256, 640)[:, :576], wout_ref[...], preferred_element_type=F32
    )
    result = result + bout_ref[...].reshape(1, 1152) + resid[...].reshape(256, 1152).astype(F32)
    out_ref[...] = result.astype(BF16).reshape(8, 32, 1152)


def shards(
    features,
    norm_gain,
    head_weight,
    head_bias,
    frame_order,
    patch_weight,
    patch_bias,
    pos_embed,
    ln_gain,
    ln_bias,
    w_qkv,
    b_qkv,
    w_out,
    b_out,
):
    hbm = pl.BlockSpec(memory_space=pl.ANY)
    vmem = pl.BlockSpec(memory_space=pltpu.VMEM)
    return pl.pallas_call(
        kernel,
        out_shape=jax.ShapeDtypeStruct((8, 32, 1152), BF16),
        in_specs=[hbm] * 18,
        out_specs=vmem,
        scratch_shapes=[
            pltpu.VMEM((8, 7, 192, 224), BF16),
            pltpu.VMEM((3, 27, 192), BF16),
            pltpu.VMEM((192,), F32),
            pltpu.SMEM((3,), F32),
            pltpu.SMEM((32,), jnp.int32),
            pltpu.VMEM((192, 224), BF16),
            pltpu.VMEM((64, 64), BF16),
            pltpu.VMEM((224, 256), BF16),
            pltpu.VMEM((640, 588), BF16),
            pltpu.VMEM((32, 1152), BF16),
            pltpu.VMEM((588, 1152), BF16),
            pltpu.VMEM((1152,), F32),
            pltpu.VMEM((1152,), F32),
            pltpu.VMEM((1152,), F32),
            pltpu.VMEM((1728, 1152), BF16),
            pltpu.VMEM((1728,), F32),
            pltpu.VMEM((576, 1152), BF16),
            pltpu.VMEM((1152,), F32),
            pltpu.VMEM((3, 32, 192), F32),
            pltpu.VMEM((10, 224, 256), F32),
            pltpu.VMEM((10, 2, 48, 256), F32),
            pltpu.VMEM((10, 2, 8, 256), F32),
            pltpu.VMEM((10, 2, 8, 256), F32),
            pltpu.VMEM((2, 2, 48, 256), F32),
            pltpu.VMEM((2, 2, 8, 256), F32),
            pltpu.VMEM((2, 2, 8, 256), F32),
            pltpu.VMEM((8, 2, 8, 256), F32),
            pltpu.VMEM((8, 2, 8, 256), F32),
            pltpu.VMEM((640, 1152), BF16),
            pltpu.VMEM((32, 16, 640), BF16),
            pltpu.VMEM((32, 16, 640), BF16),
            pltpu.VMEM((8, 32, 1152), BF16),
            pltpu.VMEM((2, 8, 16, 640), BF16),
            pltpu.VMEM((2, 8, 16, 640), BF16),
            pltpu.VMEM((8, 32, 1152), BF16),
            pltpu.VMEM((2, 128, 1152), BF16),
            pltpu.VMEM((2, 8, 3, 80, 128), BF16),
            pltpu.VMEM((2, 8, 3, 80, 128), BF16),
            pltpu.VMEM((2048, 80), BF16),
            pltpu.VMEM((80, 2048), BF16),
            pltpu.VMEM((8, 80, 256), BF16),
            pltpu.VMEM((8, 80, 256), BF16),
            pltpu.VMEM((8, 32, 640), BF16),
            pltpu.VMEM((8, 32, 640), BF16),
            pltpu.SemaphoreType.DMA((10,)),
            pltpu.SemaphoreType.DMA((17,)),
            pltpu.SemaphoreType.DMA((5,)),
            pltpu.SemaphoreType.DMA((5,)),
            pltpu.SemaphoreType.DMA((2, 3, 8)),
            pltpu.SemaphoreType.DMA((2, 3, 8)),
            pltpu.SemaphoreType.DMA((2, 4)),
            pltpu.SemaphoreType.DMA((2, 4)),
            pltpu.SemaphoreType.DMA((70,)),
            pltpu.SemaphoreType.DMA((70,)),
        ],
        compiler_params=pltpu.CompilerParams(
            collective_id=0, has_side_effects=True, vmem_limit_bytes=60 * 1024 * 1024
        ),
        name="decoder_block",
    )(
        jnp.transpose(features, (0, 1, 3, 2)),
        jnp.transpose(head_weight, (0, 2, 1)),
        norm_gain,
        head_bias,
        frame_order,
        combine_matrix(),
        edge_matrix(),
        column_matrix(),
        order_matrix(),
        pos_embed,
        patch_weight,
        patch_bias,
        ln_gain,
        ln_bias,
        w_qkv.T,
        b_qkv,
        w_out,
        b_out,
    )


def solution(mesh):
    in_specs = (
        P("ta", "ha", None, None),
        P(),
        P(),
        P(),
        P(),
        P(),
        P(),
        P("ha", None),
        P(),
        P(),
        P(),
        P(),
        P(),
        P(),
    )
    out_specs = P("ta", "ha", None)
    return jax.shard_map(shards, mesh=mesh, in_specs=in_specs, out_specs=out_specs, check_vma=False)
```

```python
import functools

import jax
import jax.numpy as jnp
import numpy as np
from jax import lax
from jax.experimental import pallas as pl
from jax.experimental.pallas import tpu as pltpu
from jax.sharding import PartitionSpec as P

HEADS = 8
HD = 72
MESH = pl.DeviceIdType.MESH
F32 = jnp.float32
BF16 = jnp.bfloat16

P_ORDER = [0, 13] + list(range(1, 13))


def shifted(g, j):
    return 1 if (g == 0 and j == 0) or (g == 1 and j == 2) else 0


def combine_matrix():
    m = np.zeros((192, 224), np.float32)
    for g in range(2):
        for j in range(3):
            base = shifted(g, j) * 96 + g * 48
            for c in range(3):
                for at, p in enumerate(P_ORDER):
                    r, h = divmod(p, 2)
                    for i in range(3):
                        source = r + (h + i - 1) // 2
                        if 0 <= source < 7:
                            m[base + at * 3 + c, source * 32 + 9 * i + 3 * j + c] = 1
    return m.astype(jnp.bfloat16)


def edge_matrix():
    m = np.zeros((64, 64), np.float32)
    for g in range(2):
        for j in range(3):
            base = shifted(g, j) * 32 + g * 16
            for c in range(3):
                m[base + c, 32 + 3 * j + c] = 1
                m[base + 8 + 3 + c, 18 + 3 * j + c] = 1
    return m.astype(jnp.bfloat16)


def column_matrix():
    m = np.zeros((224, 256), np.float32)
    for x in range(7):
        for token in range(32):
            m[x * 32 + token, 7 * token + x] = 1
    return m.astype(jnp.bfloat16)


def order_matrix():
    m = np.zeros((640, 588), np.float32)
    for q in range(14):
        for at, p in enumerate(P_ORDER):
            for c in range(3):
                m[q * 42 + at * 3 + c, 3 * (14 * p + q) + c] = 1
    return m.astype(jnp.bfloat16)


def remote(src, dst, send, recv, peer):
    return pltpu.make_async_remote_copy(
        src_ref=src, dst_ref=dst, send_sem=send, recv_sem=recv, device_id=peer, device_id_type=MESH
    )


def kernel(
    x_hbm,
    taps_hbm,
    gain_hbm,
    bias_hbm,
    order_hbm,
    combine_hbm,
    edge_hbm,
    column_hbm,
    perm_hbm,
    pos_hbm,
    pw_hbm,
    pb_hbm,
    lng_hbm,
    lnb_hbm,
    wqkv_hbm,
    bqkv_hbm,
    wout_hbm,
    bout_hbm,
    out_ref,
    x_ref,
    taps_ref,
    gain_ref,
    bias_ref,
    order_ref,
    combine_ref,
    edge_ref,
    column_ref,
    perm_ref,
    pos_ref,
    pw_ref,
    pb_ref,
    lng_ref,
    lnb_ref,
    wqkv_ref,
    bqkv_ref,
    wout_ref,
    bout_ref,
    w_ref,
    acc,
    vs,
    edn,
    eup,
    vin,
    edn_c,
    eup_c,
    edn_in,
    eup_in,
    pw_all,
    gathered_a,
    gathered_b,
    own_ref,
    x_in,
    resid,
    normed,
    q_out,
    q_in,
    k_all,
    v_all,
    c_out,
    c_in,
    z_out,
    z_in,
    x_sem,
    load_sem,
    near_send,
    near_recv,
    ring_send,
    ring_recv,
    send_sem,
    recv_sem,
):
    s = lax.axis_index("ha")
    t = lax.axis_index("ta")
    z = s // 8
    q = s % 8
    below = lax.rem(s + 1, 64)
    above = lax.rem(s + 63, 64)
    after = lax.rem(t + 1, 4)
    prior = lax.rem(t + 3, 4)

    names = [
        "taps",
        "gain",
        "bias",
        "order",
        "combine",
        "edge",
        "column",
        "perm",
        "pos",
        "pw",
        "pb",
        "lng",
        "lnb",
        "wqkv",
        "bqkv",
        "wout",
        "bout",
    ]
    sources = [
        (taps_hbm, taps_ref),
        (gain_hbm, gain_ref),
        (bias_hbm, bias_ref),
        (order_hbm, order_ref),
        (combine_hbm, combine_ref),
        (edge_hbm, edge_ref),
        (column_hbm, column_ref),
        (perm_hbm, perm_ref),
        (pos_hbm, pos_ref),
        (pw_hbm, pw_ref),
        (pb_hbm, pb_ref),
        (lng_hbm, lng_ref),
        (lnb_hbm, lnb_ref),
        (wqkv_hbm, wqkv_ref),
        (bqkv_hbm, bqkv_ref),
        (wout_hbm, wout_ref),
        (bout_hbm, bout_ref),
    ]
    loads = {
        name: pltpu.make_async_copy(source, target, load_sem.at[at])
        for at, (name, (source, target)) in enumerate(zip(names, sources))
    }

    def ready(*wanted):
        for name in wanted:
            loads.pop(name).wait()

    loads["taps"].start()
    loads["gain"].start()
    rows_in = [
        pltpu.make_async_copy(x_hbm.at[:, r], x_ref.at[:, r], x_sem.at[at])
        for at, r in ((8, 0), (9, 6))
    ]

    def inner(f):
        return pltpu.make_async_copy(
            x_hbm.at[f, pl.ds(1, 5)], x_ref.at[f, pl.ds(1, 5)], x_sem.at[f]
        )

    for copy in rows_in:
        copy.start()
    loads["edge"].start()
    for f in [6, 7, 0, 1, 2, 3, 4, 5]:
        inner(f).start()
    for name in names[2:]:
        if name != "edge":
            loads[name].start()

    planes = [lax.rem(z + d, 8) for d in range(1, 8)]
    heads = [lax.rem(q + d, 8) for d in range(1, 8)]
    ring = [{"ha": s, "ta": lax.rem(t + d, 4)} for d in range(1, 4)]
    column = [{"ha": plane * 8 + q, "ta": t} for plane in planes]
    cluster = [{"ha": z * 8 + head, "ta": t} for head in heads]
    near = [
        {"ha": below, "ta": t},
        {"ha": above, "ta": t},
        {"ha": below, "ta": after},
        {"ha": above, "ta": after},
        {"ha": below, "ta": prior},
        {"ha": above, "ta": prior},
    ]

    peers = ring + column + cluster + near
    barrier = pltpu.get_barrier_semaphore()
    for peer in peers:
        pl.semaphore_signal(barrier, inc=1, device_id=peer, device_id_type=MESH)

    w_ref[...] = jnp.zeros_like(w_ref)
    ready("taps", "gain")
    for tap in range(3):
        w_ref[tap, 0:27, :] = taps_ref[tap].astype(F32)
    acc[...] = jnp.zeros_like(acc)
    gain = jnp.transpose(jnp.broadcast_to(0.5 * gain_ref[...].reshape(1, 192), (8, 192)))[:, 0:1]
    weight = w_ref[...].reshape(96, 192).astype(BF16)

    def convolve(f, which):
        for r in which:
            x = x_ref[f, r].astype(F32)
            factor = lax.rsqrt(jnp.sum(x * x, axis=0, keepdims=True) * (1.0 / 192.0) + 1e-06)
            u = x * factor * gain
            a = (u + u * jnp.tanh(u)).astype(BF16)
            res = jnp.dot(weight, a, preferred_element_type=F32)
            rows = pl.ds(r * 32, 32)
            acc[f, rows, 0:224] += res[64:96]
            acc[f + 1, rows, 0:224] += res[32:64]
            acc[f + 2, rows, 0:224] += res[0:32]

    def combine(f):
        total = acc[f]
        high = total.astype(BF16)
        low = (total - high.astype(F32)).astype(BF16)
        m = combine_ref[...]
        y = jnp.dot(m, high, preferred_element_type=F32) + jnp.dot(
            m, low, preferred_element_type=F32
        )
        for g in range(2):
            moved = pltpu.roll(y[96 + 48 * g : 144 + 48 * g], 1 if g == 0 else 255, 1)
            vs[f, g] = y[48 * g : 48 * g + 48] + moved

    def edge_rows(f, carry):
        total = jnp.concatenate([acc[f, 0:32], acc[f, 192:224]], axis=0)
        high = total.astype(BF16)
        low = (total - high.astype(F32)).astype(BF16)
        m = edge_ref[...]
        y = jnp.dot(m, high, preferred_element_type=F32) + jnp.dot(
            m, low, preferred_element_type=F32
        )
        for g in range(2):
            moved = pltpu.roll(y[32 + 16 * g : 48 + 16 * g], 1 if g == 0 else 255, 1)
            v = y[16 * g : 16 * g + 16] + moved
            edn[f, g] = v[0:8]
            eup[f, g] = v[8:16]
        return carry

    def outer_rows(f, carry):
        convolve(f, (0, 6))
        return carry

    def inner_rows(f, carry):
        inner(f).wait()
        convolve(f, (1, 2, 3, 4, 5))
        return carry

    colour = lax.rem(lax.broadcasted_iota(jnp.int32, (48, 256), 0), 3)
    from_above = s > 0
    from_below = s < 63
    from_prior = t > 0

    gathered = (gathered_a, gathered_b)

    def spread(half, f):
        slot = t * 8 + f
        return [
            remote(
                gathered[half].at[slot],
                gathered[half].at[slot],
                ring_send.at[half, d, f],
                ring_recv.at[half, d, f],
                ring[d],
            )
            for d in range(3)
        ]

    def finish(f):
        bias = jnp.where(colour == 0, bias_ref[0], jnp.where(colour == 1, bias_ref[1], bias_ref[2]))
        parts = []
        for g in range(2):
            edge = jnp.where(from_above, edn_in[f, g], 0.0) + jnp.where(
                from_below, eup_in[f, g], 0.0
            )
            v = vs[f, g] + bias
            parts += [v[0:8] + edge, v[8:48]]
        v = jnp.concatenate(parts, axis=0).astype(BF16)
        cols = lax.dot_general(
            column_ref[...], v, (((1,), (1,)), ((), ())), preferred_element_type=F32
        )
        pieces = [
            cols[x * 32 : (x + 1) * 32, g * 48 : g * 48 + 42] for x in range(7) for g in range(2)
        ]
        pieces.append(jnp.zeros((32, 52), F32))
        tokens = jnp.concatenate(pieces, axis=1).astype(BF16)
        for half in range(2):
            gathered[half][t * 8 + f] = tokens[16 * half : 16 * half + 16]
        for copy in spread(0, f):
            copy.start()

    for copy in rows_in:
        copy.wait()
    lax.fori_loop(0, 8, outer_rows, 0)
    ready("edge")
    lax.fori_loop(0, 10, edge_rows, 0)
    tail = pl.ds(8, 2)
    body = pl.ds(0, 8)
    halo = [
        remote(edn.at[body], edn_in, near_send.at[0], near_recv.at[0], near[0]),
        remote(eup.at[body], eup_in, near_send.at[1], near_recv.at[1], near[1]),
        remote(edn.at[tail], edn_c, near_send.at[2], near_recv.at[2], near[2]),
        remote(eup.at[tail], eup_c, near_send.at[3], near_recv.at[3], near[3]),
        remote(vs.at[tail], vin, near_send.at[4], near_recv.at[4], {"ha": s, "ta": after}),
    ]
    pl.semaphore_wait(barrier, len(peers))
    for copy in halo[:4]:
        copy.start()
    lax.fori_loop(6, 8, inner_rows, 0)
    ready("combine")
    for f in (8, 9):
        combine(f)
    halo[4].start()
    lax.fori_loop(0, 2, inner_rows, 0)
    ready("bias", "column")
    lax.fori_loop(2, 3, inner_rows, 0)
    for f in range(3):
        combine(f)
    for copy in halo:
        copy.wait()
    for first in range(2):
        for g in range(2):
            extra = jnp.where(from_prior, vin[first, g], 0.0)
            corner = jnp.where(from_prior & from_above, edn_c[first, g], 0.0) + jnp.where(
                from_prior & from_below, eup_c[first, g], 0.0
            )
            vs[first, g] += extra
            vs[first, g, 0:8] += corner

    def finish_one(f, carry):
        finish(f)
        return carry

    def early(f, carry):
        inner_rows(f, carry)
        combine(f)
        finish(f)
        return carry

    lax.fori_loop(0, 3, finish_one, 0)
    lax.fori_loop(3, 6, early, 0)
    for f in (6, 7):
        combine(f)
    lax.fori_loop(6, 8, finish_one, 0)
    for f in range(8):
        for copy in spread(1, f):
            copy.start()
    ready("perm", "pw", "order", "pos")
    pw_all[...] = jnp.dot(perm_ref[...], pw_ref[...], preferred_element_type=F32).astype(BF16)
    row = lax.broadcasted_iota(jnp.int32, (80, 128), 0)
    for half in range(2):
        for h in range(8):
            q_out[half, h, 0] = jnp.zeros((80, 128), BF16)
            q_out[half, h, 1] = jnp.zeros((80, 128), BF16)
            q_out[half, h, 2] = jnp.where(row == HD, 1.0, 0.0).astype(BF16)
    z_out[...] = jnp.zeros_like(z_out)
    ready("pb", "lng", "lnb", "bqkv", "wqkv")
    qkv_bias = jnp.transpose(jnp.broadcast_to(bqkv_ref[...].reshape(1, 1728), (8, 1728)))[:, 0:1]

    def frames(half):
        return [
            remote(
                resid.at[half, planes[d]],
                x_in.at[half, z],
                send_sem.at[7 * half + d],
                recv_sem.at[7 * half + d],
                column[d],
            )
            for d in range(7)
        ]

    def exchange(half):
        for f in range(8):
            for copy in spread(half, f):
                copy.wait()
        for j in range(8):
            own_ref[half, j] = gathered[half][order_ref[t * 8 + j]]
        here = slice(16 * half, 16 * half + 16)
        value = jnp.dot(
            own_ref[half].reshape(128, 640), pw_all[...], preferred_element_type=F32
        ).reshape(8, 16, 1152)
        value = value + pb_ref[...].reshape(1, 1, 1152)
        resid[half] = (value + pos_ref[here, :].reshape(1, 16, 1152).astype(F32)).astype(BF16)
        for copy in frames(half):
            copy.start()
        x_in[half, z] = resid[half, z]

    def normalise(half):
        for copy in frames(half):
            copy.wait()
        value = x_in[half].reshape(128, 1152).astype(F32)
        centre = jnp.mean(value, axis=-1, keepdims=True)
        value = value - centre
        spread_out = jnp.mean(value * value, axis=-1, keepdims=True)
        normed[half] = (
            value * lax.rsqrt(spread_out + 1e-06) * lng_ref[...].reshape(1, 1152)
            + lnb_ref[...].reshape(1, 1152)
        ).astype(BF16)

    def pair(half, kind, d):
        at = 14 + half * 21 + kind * 7 + d
        return remote(
            q_out.at[half, heads[d], kind],
            q_in.at[half, q, kind],
            send_sem.at[at],
            recv_sem.at[at],
            cluster[d],
        )

    def project(half):
        for kind in (1, 0, 2):
            rows = slice(kind * 576, kind * 576 + 576)
            made = (
                lax.dot_general(
                    wqkv_ref[rows, :],
                    normed[half],
                    (((1,), (1,)), ((), ())),
                    preferred_element_type=F32,
                )
                + qkv_bias[rows]
            )
            for h in range(8):
                q_out[half, h, kind, 0:HD] = made[h * HD : (h + 1) * HD].astype(BF16)
            for d in range(7):
                pair(half, kind, d).start()
            q_in[half, q, kind] = q_out[half, q, kind]

    exchange(0)
    normalise(0)
    exchange(1)
    project(0)
    normalise(1)
    project(1)
    for half in range(2):
        for d in range(7):
            pair(half, 1, d).wait()
        for p in range(8):
            at = half * 1024 + p * 128
            k_all[at : at + 128, :] = jnp.transpose(q_in[half, p, 1].astype(F32)).astype(BF16)
        for d in range(7):
            pair(half, 0, d).wait()
    for half in range(2):
        for d in range(7):
            pair(half, 2, d).wait()
        for p in range(8):
            at = half * 1024 + p * 128
            v_all[:, at : at + 128] = q_in[half, p, 2]

    rate = HD ** (-0.5) * 1.4426950408889634

    def attend(i, carry):
        p = lax.rem(q + 1 + i, 8)
        asked = jnp.concatenate([q_in[0, p, 0], q_in[1, p, 0]], axis=1)
        scores = jnp.dot(k_all[...], asked, preferred_element_type=F32)
        highest = jnp.max(scores, axis=0, keepdims=True)
        weights = jnp.exp2((scores - highest) * rate).astype(BF16)
        mixed = jnp.dot(v_all[...], weights, preferred_element_type=F32)
        c_out[p] = (mixed / mixed[HD : HD + 1]).astype(BF16)

        @pl.when(i < 7)
        def _():
            remote(
                c_out.at[p],
                c_in.at[q],
                send_sem.at[56 + i],
                recv_sem.at[56 + i],
                {"ha": z * 8 + p, "ta": t},
            ).start()

        return carry

    lax.fori_loop(0, 8, attend, 0)
    c_in[q] = c_out[q]
    for d in range(7):
        remote(
            c_out.at[heads[d]], c_in.at[q], send_sem.at[56 + d], recv_sem.at[56 + d], cluster[d]
        ).wait()
    sides = jnp.concatenate([c_in[h, 0:HD].astype(F32) for h in range(8)], axis=0)
    merged = jnp.transpose(sides).astype(BF16).reshape(2, 8, 16, 576)
    for half in range(2):
        z_out[:, 16 * half : 16 * half + 16, 0:576] = merged[half]
    backs = []
    for d in range(7):
        copy = remote(
            z_out.at[planes[d]], z_in.at[z], send_sem.at[63 + d], recv_sem.at[63 + d], column[d]
        )
        copy.start()
        backs.append(copy)
    z_in[z] = z_out[z]
    ready("wout", "bout")
    for copy in backs:
        copy.wait()
    result = jnp.dot(
        z_in[...].reshape(256, 640)[:, :576], wout_ref[...], preferred_element_type=F32
    )
    result = (result + bout_ref[...].reshape(1, 1152)).reshape(8, 32, 1152)
    for half in range(2):
        here = slice(16 * half, 16 * half + 16)
        out_ref[:, here, :] = (result[:, here, :] + resid[half].astype(F32)).astype(BF16)


def shards(
    features,
    norm_gain,
    head_weight,
    head_bias,
    frame_order,
    patch_weight,
    patch_bias,
    pos_embed,
    ln_gain,
    ln_bias,
    w_qkv,
    b_qkv,
    w_out,
    b_out,
):
    hbm = pl.BlockSpec(memory_space=pl.ANY)
    vmem = pl.BlockSpec(memory_space=pltpu.VMEM)
    return pl.pallas_call(
        kernel,
        out_shape=jax.ShapeDtypeStruct((8, 32, 1152), BF16),
        in_specs=[hbm] * 18,
        out_specs=vmem,
        scratch_shapes=[
            pltpu.VMEM((8, 7, 192, 224), BF16),
            pltpu.VMEM((3, 27, 192), BF16),
            pltpu.VMEM((192,), F32),
            pltpu.SMEM((3,), F32),
            pltpu.SMEM((32,), jnp.int32),
            pltpu.VMEM((192, 224), BF16),
            pltpu.VMEM((64, 64), BF16),
            pltpu.VMEM((224, 256), BF16),
            pltpu.VMEM((640, 588), BF16),
            pltpu.VMEM((32, 1152), BF16),
            pltpu.VMEM((588, 1152), BF16),
            pltpu.VMEM((1152,), F32),
            pltpu.VMEM((1152,), F32),
            pltpu.VMEM((1152,), F32),
            pltpu.VMEM((1728, 1152), BF16),
            pltpu.VMEM((1728,), F32),
            pltpu.VMEM((576, 1152), BF16),
            pltpu.VMEM((1152,), F32),
            pltpu.VMEM((3, 32, 192), F32),
            pltpu.VMEM((10, 224, 256), F32),
            pltpu.VMEM((10, 2, 48, 256), F32),
            pltpu.VMEM((10, 2, 8, 256), F32),
            pltpu.VMEM((10, 2, 8, 256), F32),
            pltpu.VMEM((2, 2, 48, 256), F32),
            pltpu.VMEM((2, 2, 8, 256), F32),
            pltpu.VMEM((2, 2, 8, 256), F32),
            pltpu.VMEM((8, 2, 8, 256), F32),
            pltpu.VMEM((8, 2, 8, 256), F32),
            pltpu.VMEM((640, 1152), BF16),
            pltpu.VMEM((32, 16, 640), BF16),
            pltpu.VMEM((32, 16, 640), BF16),
            pltpu.VMEM((2, 8, 16, 640), BF16),
            pltpu.VMEM((2, 8, 16, 1152), BF16),
            pltpu.VMEM((2, 8, 16, 1152), BF16),
            pltpu.VMEM((2, 128, 1152), BF16),
            pltpu.VMEM((2, 8, 3, 80, 128), BF16),
            pltpu.VMEM((2, 8, 3, 80, 128), BF16),
            pltpu.VMEM((2048, 80), BF16),
            pltpu.VMEM((80, 2048), BF16),
            pltpu.VMEM((8, 80, 256), BF16),
            pltpu.VMEM((8, 80, 256), BF16),
            pltpu.VMEM((8, 32, 640), BF16),
            pltpu.VMEM((8, 32, 640), BF16),
            pltpu.SemaphoreType.DMA((10,)),
            pltpu.SemaphoreType.DMA((17,)),
            pltpu.SemaphoreType.DMA((5,)),
            pltpu.SemaphoreType.DMA((5,)),
            pltpu.SemaphoreType.DMA((2, 3, 8)),
            pltpu.SemaphoreType.DMA((2, 3, 8)),
            pltpu.SemaphoreType.DMA((70,)),
            pltpu.SemaphoreType.DMA((70,)),
        ],
        compiler_params=pltpu.CompilerParams(
            collective_id=0, has_side_effects=True, vmem_limit_bytes=60 * 1024 * 1024
        ),
        name="decoder_block",
    )(
        jnp.transpose(features, (0, 1, 3, 2)),
        jnp.transpose(head_weight, (0, 2, 1)),
        norm_gain,
        head_bias,
        frame_order,
        combine_matrix(),
        edge_matrix(),
        column_matrix(),
        order_matrix(),
        pos_embed,
        patch_weight,
        patch_bias,
        ln_gain,
        ln_bias,
        w_qkv.T,
        b_qkv,
        w_out,
        b_out,
    )


def solution(mesh):
    in_specs = (
        P("ta", "ha", None, None),
        P(),
        P(),
        P(),
        P(),
        P(),
        P(),
        P("ha", None),
        P(),
        P(),
        P(),
        P(),
        P(),
        P(),
    )
    out_specs = P("ta", "ha", None)
    return jax.shard_map(shards, mesh=mesh, in_specs=in_specs, out_specs=out_specs, check_vma=False)
```

```python
import functools

import jax
import jax.numpy as jnp
import numpy as np
from jax import lax
from jax.experimental import pallas as pl
from jax.experimental.pallas import tpu as pltpu
from jax.sharding import PartitionSpec as P

HEADS = 8
HD = 72
MESH = pl.DeviceIdType.MESH
F32 = jnp.float32
BF16 = jnp.bfloat16

P_ORDER = [0, 13] + list(range(1, 13))


def shifted(g, j):
    return 1 if (g == 0 and j == 0) or (g == 1 and j == 2) else 0


def combine_matrix():
    m = np.zeros((192, 224), np.float32)
    for g in range(2):
        for j in range(3):
            base = shifted(g, j) * 96 + g * 48
            for c in range(3):
                for at, p in enumerate(P_ORDER):
                    r, h = divmod(p, 2)
                    for i in range(3):
                        source = r + (h + i - 1) // 2
                        if 0 <= source < 7:
                            m[base + at * 3 + c, source * 32 + 9 * i + 3 * j + c] = 1
    return m.astype(jnp.bfloat16)


def edge_matrix():
    m = np.zeros((64, 64), np.float32)
    for g in range(2):
        for j in range(3):
            base = shifted(g, j) * 32 + g * 16
            for c in range(3):
                m[base + c, 32 + 3 * j + c] = 1
                m[base + 8 + 3 + c, 18 + 3 * j + c] = 1
    return m.astype(jnp.bfloat16)


def column_matrix():
    m = np.zeros((224, 256), np.float32)
    for x in range(7):
        for token in range(32):
            m[x * 32 + token, 7 * token + x] = 1
    return m.astype(jnp.bfloat16)


def order_matrix():
    m = np.zeros((640, 588), np.float32)
    for q in range(14):
        for at, p in enumerate(P_ORDER):
            for c in range(3):
                m[q * 42 + at * 3 + c, 3 * (14 * p + q) + c] = 1
    return m.astype(jnp.bfloat16)


def remote(src, dst, send, recv, peer):
    return pltpu.make_async_remote_copy(
        src_ref=src, dst_ref=dst, send_sem=send, recv_sem=recv, device_id=peer, device_id_type=MESH
    )


def kernel(
    x_hbm,
    taps_hbm,
    gain_hbm,
    bias_hbm,
    order_hbm,
    combine_hbm,
    edge_hbm,
    column_hbm,
    perm_hbm,
    pos_hbm,
    pw_hbm,
    pb_hbm,
    lng_hbm,
    lnb_hbm,
    wqkv_hbm,
    bqkv_hbm,
    wout_hbm,
    bout_hbm,
    out_ref,
    x_ref,
    taps_ref,
    gain_ref,
    bias_ref,
    order_ref,
    combine_ref,
    edge_ref,
    column_ref,
    perm_ref,
    pos_ref,
    pw_ref,
    pb_ref,
    lng_ref,
    lnb_ref,
    wqkv_ref,
    bqkv_ref,
    wout_ref,
    bout_ref,
    w_ref,
    acc,
    vs,
    edn,
    eup,
    vin,
    edn_c,
    eup_c,
    edn_in,
    eup_in,
    pw_all,
    gathered_a,
    gathered_b,
    pos_in,
    own_ref,
    x_in,
    resid,
    normed,
    q_out,
    q_in,
    k_all,
    v_all,
    c_out,
    c_in,
    z_out,
    z_in,
    x_sem,
    load_sem,
    near_send,
    near_recv,
    ring_send,
    ring_recv,
    pos_send,
    pos_recv,
    send_sem,
    recv_sem,
):
    s = lax.axis_index("ha")
    t = lax.axis_index("ta")
    z = s // 8
    q = s % 8
    below = lax.rem(s + 1, 64)
    above = lax.rem(s + 63, 64)
    after = lax.rem(t + 1, 4)
    prior = lax.rem(t + 3, 4)

    names = [
        "taps",
        "gain",
        "bias",
        "order",
        "combine",
        "edge",
        "column",
        "perm",
        "pos",
        "pw",
        "pb",
        "lng",
        "lnb",
        "wqkv",
        "bqkv",
        "wout",
        "bout",
    ]
    sources = [
        (taps_hbm, taps_ref),
        (gain_hbm, gain_ref),
        (bias_hbm, bias_ref),
        (order_hbm, order_ref),
        (combine_hbm, combine_ref),
        (edge_hbm, edge_ref),
        (column_hbm, column_ref),
        (perm_hbm, perm_ref),
        (pos_hbm, pos_ref),
        (pw_hbm, pw_ref),
        (pb_hbm, pb_ref),
        (lng_hbm, lng_ref),
        (lnb_hbm, lnb_ref),
        (wqkv_hbm, wqkv_ref),
        (bqkv_hbm, bqkv_ref),
        (wout_hbm, wout_ref),
        (bout_hbm, bout_ref),
    ]
    loads = {
        name: pltpu.make_async_copy(source, target, load_sem.at[at])
        for at, (name, (source, target)) in enumerate(zip(names, sources))
    }

    def ready(*wanted):
        for name in wanted:
            loads.pop(name).wait()

    loads["taps"].start()
    loads["gain"].start()
    rows_in = [
        pltpu.make_async_copy(x_hbm.at[:, r], x_ref.at[:, r], x_sem.at[at])
        for at, r in ((8, 0), (9, 6))
    ]

    def inner(f):
        return pltpu.make_async_copy(
            x_hbm.at[f, pl.ds(1, 5)], x_ref.at[f, pl.ds(1, 5)], x_sem.at[f]
        )

    for copy in rows_in:
        copy.start()
    loads["edge"].start()
    for f in [6, 7, 0, 1, 2, 3, 4, 5]:
        inner(f).start()
    for name in names[2:]:
        if name != "edge":
            loads[name].start()

    planes = [lax.rem(z + d, 8) for d in range(1, 8)]
    heads = [lax.rem(q + d, 8) for d in range(1, 8)]
    ring = [{"ha": s, "ta": lax.rem(t + d, 4)} for d in range(1, 4)]
    column = [{"ha": plane * 8 + q, "ta": t} for plane in planes]
    cluster = [{"ha": z * 8 + head, "ta": t} for head in heads]
    near = [
        {"ha": below, "ta": t},
        {"ha": above, "ta": t},
        {"ha": below, "ta": after},
        {"ha": above, "ta": after},
        {"ha": below, "ta": prior},
        {"ha": above, "ta": prior},
    ]

    peers = ring + column + cluster + near
    barrier = pltpu.get_barrier_semaphore()
    for peer in peers:
        pl.semaphore_signal(barrier, inc=1, device_id=peer, device_id_type=MESH)

    w_ref[...] = jnp.zeros_like(w_ref)
    ready("taps", "gain")
    for tap in range(3):
        w_ref[tap, 0:27, :] = taps_ref[tap].astype(F32)
    acc[...] = jnp.zeros_like(acc)
    gain = jnp.transpose(jnp.broadcast_to(0.5 * gain_ref[...].reshape(1, 192), (8, 192)))[:, 0:1]
    weight = w_ref[...].reshape(96, 192).astype(BF16)

    def convolve(f, which):
        for r in which:
            x = x_ref[f, r].astype(F32)
            factor = lax.rsqrt(jnp.sum(x * x, axis=0, keepdims=True) * (1.0 / 192.0) + 1e-06)
            u = x * factor * gain
            a = (u + u * jnp.tanh(u)).astype(BF16)
            res = jnp.dot(weight, a, preferred_element_type=F32)
            rows = pl.ds(r * 32, 32)
            acc[f, rows, 0:224] += res[64:96]
            acc[f + 1, rows, 0:224] += res[32:64]
            acc[f + 2, rows, 0:224] += res[0:32]

    def combine(f):
        total = acc[f]
        high = total.astype(BF16)
        low = (total - high.astype(F32)).astype(BF16)
        m = combine_ref[...]
        y = jnp.dot(m, high, preferred_element_type=F32) + jnp.dot(
            m, low, preferred_element_type=F32
        )
        for g in range(2):
            moved = pltpu.roll(y[96 + 48 * g : 144 + 48 * g], 1 if g == 0 else 255, 1)
            vs[f, g] = y[48 * g : 48 * g + 48] + moved

    def edge_rows(f, carry):
        total = jnp.concatenate([acc[f, 0:32], acc[f, 192:224]], axis=0)
        high = total.astype(BF16)
        low = (total - high.astype(F32)).astype(BF16)
        m = edge_ref[...]
        y = jnp.dot(m, high, preferred_element_type=F32) + jnp.dot(
            m, low, preferred_element_type=F32
        )
        for g in range(2):
            moved = pltpu.roll(y[32 + 16 * g : 48 + 16 * g], 1 if g == 0 else 255, 1)
            v = y[16 * g : 16 * g + 16] + moved
            edn[f, g] = v[0:8]
            eup[f, g] = v[8:16]
        return carry

    def outer_rows(f, carry):
        convolve(f, (0, 6))
        return carry

    def inner_rows(f, carry):
        inner(f).wait()
        convolve(f, (1, 2, 3, 4, 5))
        return carry

    colour = lax.rem(lax.broadcasted_iota(jnp.int32, (48, 256), 0), 3)
    from_above = s > 0
    from_below = s < 63
    from_prior = t > 0

    gathered = (gathered_a, gathered_b)

    def spread(half, f):
        slot = t * 8 + f
        return [
            remote(
                gathered[half].at[slot],
                gathered[half].at[slot],
                ring_send.at[half, d, f],
                ring_recv.at[half, d, f],
                ring[d],
            )
            for d in range(3)
        ]

    def finish(f):
        bias = jnp.where(colour == 0, bias_ref[0], jnp.where(colour == 1, bias_ref[1], bias_ref[2]))
        parts = []
        for g in range(2):
            edge = jnp.where(from_above, edn_in[f, g], 0.0) + jnp.where(
                from_below, eup_in[f, g], 0.0
            )
            v = vs[f, g] + bias
            parts += [v[0:8] + edge, v[8:48]]
        v = jnp.concatenate(parts, axis=0).astype(BF16)
        cols = lax.dot_general(
            column_ref[...], v, (((1,), (1,)), ((), ())), preferred_element_type=F32
        )
        pieces = [
            cols[x * 32 : (x + 1) * 32, g * 48 : g * 48 + 42] for x in range(7) for g in range(2)
        ]
        pieces.append(jnp.zeros((32, 52), F32))
        tokens = jnp.concatenate(pieces, axis=1).astype(BF16)
        for half in range(2):
            gathered[half][t * 8 + f] = tokens[16 * half : 16 * half + 16]
        for copy in spread(0, f):
            copy.start()

    right = {"ha": lax.rem(z + 1, 8) * 8 + q, "ta": t}
    left = {"ha": lax.rem(z + 7, 8) * 8 + q, "ta": t}

    def relay(k, way):
        slot = lax.rem(z + 8 - k, 8) if way == 0 else lax.rem(z + k, 8)
        return remote(
            pos_in.at[slot],
            pos_in.at[slot],
            pos_send.at[way, k],
            pos_recv.at[way, k],
            right if way == 0 else left,
        )

    def relay_start(k):
        for way in (0, 1) if k < 3 else (0,):
            relay(k, way).start()

    def relay_wait(k):
        for way in (0, 1) if k < 3 else (0,):
            relay(k, way).wait()

    for copy in rows_in:
        copy.wait()
    lax.fori_loop(0, 8, outer_rows, 0)
    ready("edge", "pos")
    lax.fori_loop(0, 10, edge_rows, 0)
    pos_in[z] = pos_ref[...]
    tail = pl.ds(8, 2)
    body = pl.ds(0, 8)
    halo = [
        remote(edn.at[body], edn_in, near_send.at[0], near_recv.at[0], near[0]),
        remote(eup.at[body], eup_in, near_send.at[1], near_recv.at[1], near[1]),
        remote(edn.at[tail], edn_c, near_send.at[2], near_recv.at[2], near[2]),
        remote(eup.at[tail], eup_c, near_send.at[3], near_recv.at[3], near[3]),
        remote(vs.at[tail], vin, near_send.at[4], near_recv.at[4], {"ha": s, "ta": after}),
    ]
    pl.semaphore_wait(barrier, len(peers))
    for copy in halo[:4]:
        copy.start()
    relay_start(0)
    lax.fori_loop(6, 8, inner_rows, 0)
    ready("combine")
    for f in (8, 9):
        combine(f)
    halo[4].start()
    lax.fori_loop(0, 2, inner_rows, 0)
    ready("bias", "column")
    lax.fori_loop(2, 3, inner_rows, 0)
    for f in range(3):
        combine(f)
    for copy in halo:
        copy.wait()
    for first in range(2):
        for g in range(2):
            extra = jnp.where(from_prior, vin[first, g], 0.0)
            corner = jnp.where(from_prior & from_above, edn_c[first, g], 0.0) + jnp.where(
                from_prior & from_below, eup_c[first, g], 0.0
            )
            vs[first, g] += extra
            vs[first, g, 0:8] += corner

    def finish_one(f, carry):
        finish(f)
        return carry

    def early(f, carry):
        inner_rows(f, carry)
        combine(f)
        finish(f)
        return carry

    lax.fori_loop(0, 3, finish_one, 0)
    relay_wait(0)
    relay_start(1)
    lax.fori_loop(3, 6, early, 0)
    relay_wait(1)
    relay_start(2)
    for f in (6, 7):
        combine(f)
    lax.fori_loop(6, 8, finish_one, 0)
    relay_wait(2)
    relay_start(3)
    for f in range(8):
        for copy in spread(1, f):
            copy.start()
    ready("perm", "pw", "order")
    pw_all[...] = jnp.dot(perm_ref[...], pw_ref[...], preferred_element_type=F32).astype(BF16)
    row = lax.broadcasted_iota(jnp.int32, (80, 128), 0)
    for half in range(2):
        for h in range(8):
            q_out[half, h, 0] = jnp.zeros((80, 128), BF16)
            q_out[half, h, 1] = jnp.zeros((80, 128), BF16)
            q_out[half, h, 2] = jnp.where(row == HD, 1.0, 0.0).astype(BF16)
    z_out[...] = jnp.zeros_like(z_out)
    ready("pb", "lng", "lnb", "bqkv", "wqkv")
    qkv_bias = jnp.transpose(jnp.broadcast_to(bqkv_ref[...].reshape(1, 1728), (8, 1728)))[:, 0:1]

    def frames(half):
        return [
            remote(
                own_ref.at[half, planes[d]],
                x_in.at[half, z],
                send_sem.at[7 * half + d],
                recv_sem.at[7 * half + d],
                column[d],
            )
            for d in range(7)
        ]

    def exchange(half):
        for f in range(8):
            for copy in spread(half, f):
                copy.wait()
        for j in range(8):
            own_ref[half, j] = gathered[half][order_ref[t * 8 + j]]
        for copy in frames(half):
            copy.start()
        x_in[half, z] = own_ref[half, z]

    def embed(tokens, positions):
        value = jnp.dot(
            tokens.reshape(128, 640), pw_all[...], preferred_element_type=F32
        ).reshape(8, 16, 1152)
        return (value + pb_ref[...].reshape(1, 1, 1152) + positions.astype(F32)).astype(BF16)

    def keep(half):
        here = slice(16 * half, 16 * half + 16)
        resid[:, here, :] = embed(own_ref[half], pos_ref[here, :].reshape(1, 16, 1152))

    def normalise(half):
        for copy in frames(half):
            copy.wait()
        here = slice(16 * half, 16 * half + 16)
        value = embed(x_in[half], pos_in[:, here, :]).reshape(128, 1152).astype(F32)
        centre = jnp.mean(value, axis=-1, keepdims=True)
        value = value - centre
        spread_out = jnp.mean(value * value, axis=-1, keepdims=True)
        normed[half] = (
            value * lax.rsqrt(spread_out + 1e-06) * lng_ref[...].reshape(1, 1152)
            + lnb_ref[...].reshape(1, 1152)
        ).astype(BF16)

    def pair(half, kind, d):
        at = 14 + half * 21 + kind * 7 + d
        return remote(
            q_out.at[half, heads[d], kind],
            q_in.at[half, q, kind],
            send_sem.at[at],
            recv_sem.at[at],
            cluster[d],
        )

    def project(half):
        for kind in (1, 0, 2):
            rows = slice(kind * 576, kind * 576 + 576)
            made = (
                lax.dot_general(
                    wqkv_ref[rows, :],
                    normed[half],
                    (((1,), (1,)), ((), ())),
                    preferred_element_type=F32,
                )
                + qkv_bias[rows]
            )
            for h in range(8):
                q_out[half, h, kind, 0:HD] = made[h * HD : (h + 1) * HD].astype(BF16)
            for d in range(7):
                pair(half, kind, d).start()
            q_in[half, q, kind] = q_out[half, q, kind]

    exchange(0)
    keep(0)
    relay_wait(3)
    normalise(0)
    exchange(1)
    project(0)
    keep(1)
    normalise(1)
    project(1)
    for half in range(2):
        for d in range(7):
            pair(half, 1, d).wait()
        for p in range(8):
            at = half * 1024 + p * 128
            k_all[at : at + 128, :] = jnp.transpose(q_in[half, p, 1].astype(F32)).astype(BF16)
        for d in range(7):
            pair(half, 0, d).wait()
    for half in range(2):
        for d in range(7):
            pair(half, 2, d).wait()
        for p in range(8):
            at = half * 1024 + p * 128
            v_all[:, at : at + 128] = q_in[half, p, 2]

    rate = HD ** (-0.5) * 1.4426950408889634

    def attend(i, carry):
        p = lax.rem(q + 1 + i, 8)
        asked = jnp.concatenate([q_in[0, p, 0], q_in[1, p, 0]], axis=1)
        scores = jnp.dot(k_all[...], asked, preferred_element_type=F32)
        highest = jnp.max(scores, axis=0, keepdims=True)
        weights = jnp.exp2((scores - highest) * rate).astype(BF16)
        mixed = jnp.dot(v_all[...], weights, preferred_element_type=F32)
        c_out[p] = (mixed / mixed[HD : HD + 1]).astype(BF16)

        @pl.when(i < 7)
        def _():
            remote(
                c_out.at[p],
                c_in.at[q],
                send_sem.at[56 + i],
                recv_sem.at[56 + i],
                {"ha": z * 8 + p, "ta": t},
            ).start()

        return carry

    lax.fori_loop(0, 8, attend, 0)
    c_in[q] = c_out[q]
    for d in range(7):
        remote(
            c_out.at[heads[d]], c_in.at[q], send_sem.at[56 + d], recv_sem.at[56 + d], cluster[d]
        ).wait()
    sides = jnp.concatenate([c_in[h, 0:HD].astype(F32) for h in range(8)], axis=0)
    merged = jnp.transpose(sides).astype(BF16).reshape(2, 8, 16, 576)
    for half in range(2):
        z_out[:, 16 * half : 16 * half + 16, 0:576] = merged[half]
    backs = []
    for d in range(7):
        copy = remote(
            z_out.at[planes[d]], z_in.at[z], send_sem.at[63 + d], recv_sem.at[63 + d], column[d]
        )
        copy.start()
        backs.append(copy)
    z_in[z] = z_out[z]
    ready("wout", "bout")
    for copy in backs:
        copy.wait()
    result = jnp.dot(
        z_in[...].reshape(256, 640)[:, :576], wout_ref[...], preferred_element_type=F32
    )
    result = result + bout_ref[...].reshape(1, 1152) + resid[...].reshape(256, 1152).astype(F32)
    out_ref[...] = result.astype(BF16).reshape(8, 32, 1152)


def shards(
    features,
    norm_gain,
    head_weight,
    head_bias,
    frame_order,
    patch_weight,
    patch_bias,
    pos_embed,
    ln_gain,
    ln_bias,
    w_qkv,
    b_qkv,
    w_out,
    b_out,
):
    hbm = pl.BlockSpec(memory_space=pl.ANY)
    vmem = pl.BlockSpec(memory_space=pltpu.VMEM)
    return pl.pallas_call(
        kernel,
        out_shape=jax.ShapeDtypeStruct((8, 32, 1152), BF16),
        in_specs=[hbm] * 18,
        out_specs=vmem,
        scratch_shapes=[
            pltpu.VMEM((8, 7, 192, 224), BF16),
            pltpu.VMEM((3, 27, 192), BF16),
            pltpu.VMEM((192,), F32),
            pltpu.SMEM((3,), F32),
            pltpu.SMEM((32,), jnp.int32),
            pltpu.VMEM((192, 224), BF16),
            pltpu.VMEM((64, 64), BF16),
            pltpu.VMEM((224, 256), BF16),
            pltpu.VMEM((640, 588), BF16),
            pltpu.VMEM((32, 1152), BF16),
            pltpu.VMEM((588, 1152), BF16),
            pltpu.VMEM((1152,), F32),
            pltpu.VMEM((1152,), F32),
            pltpu.VMEM((1152,), F32),
            pltpu.VMEM((1728, 1152), BF16),
            pltpu.VMEM((1728,), F32),
            pltpu.VMEM((576, 1152), BF16),
            pltpu.VMEM((1152,), F32),
            pltpu.VMEM((3, 32, 192), F32),
            pltpu.VMEM((10, 224, 256), F32),
            pltpu.VMEM((10, 2, 48, 256), F32),
            pltpu.VMEM((10, 2, 8, 256), F32),
            pltpu.VMEM((10, 2, 8, 256), F32),
            pltpu.VMEM((2, 2, 48, 256), F32),
            pltpu.VMEM((2, 2, 8, 256), F32),
            pltpu.VMEM((2, 2, 8, 256), F32),
            pltpu.VMEM((8, 2, 8, 256), F32),
            pltpu.VMEM((8, 2, 8, 256), F32),
            pltpu.VMEM((640, 1152), BF16),
            pltpu.VMEM((32, 16, 640), BF16),
            pltpu.VMEM((32, 16, 640), BF16),
            pltpu.VMEM((8, 32, 1152), BF16),
            pltpu.VMEM((2, 8, 16, 640), BF16),
            pltpu.VMEM((2, 8, 16, 640), BF16),
            pltpu.VMEM((8, 32, 1152), BF16),
            pltpu.VMEM((2, 128, 1152), BF16),
            pltpu.VMEM((2, 8, 3, 80, 128), BF16),
            pltpu.VMEM((2, 8, 3, 80, 128), BF16),
            pltpu.VMEM((2048, 80), BF16),
            pltpu.VMEM((80, 2048), BF16),
            pltpu.VMEM((8, 80, 256), BF16),
            pltpu.VMEM((8, 80, 256), BF16),
            pltpu.VMEM((8, 32, 640), BF16),
            pltpu.VMEM((8, 32, 640), BF16),
            pltpu.SemaphoreType.DMA((10,)),
            pltpu.SemaphoreType.DMA((17,)),
            pltpu.SemaphoreType.DMA((5,)),
            pltpu.SemaphoreType.DMA((5,)),
            pltpu.SemaphoreType.DMA((2, 3, 8)),
            pltpu.SemaphoreType.DMA((2, 3, 8)),
            pltpu.SemaphoreType.DMA((2, 4)),
            pltpu.SemaphoreType.DMA((2, 4)),
            pltpu.SemaphoreType.DMA((70,)),
            pltpu.SemaphoreType.DMA((70,)),
        ],
        compiler_params=pltpu.CompilerParams(
            collective_id=0, has_side_effects=True, vmem_limit_bytes=60 * 1024 * 1024
        ),
        name="decoder_block",
    )(
        jnp.transpose(features, (0, 1, 3, 2)),
        jnp.transpose(head_weight, (0, 2, 1)),
        norm_gain,
        head_bias,
        frame_order,
        combine_matrix(),
        edge_matrix(),
        column_matrix(),
        order_matrix(),
        pos_embed,
        patch_weight,
        patch_bias,
        ln_gain,
        ln_bias,
        w_qkv.T,
        b_qkv,
        w_out,
        b_out,
    )


def solution(mesh):
    in_specs = (
        P("ta", "ha", None, None),
        P(),
        P(),
        P(),
        P(),
        P(),
        P(),
        P("ha", None),
        P(),
        P(),
        P(),
        P(),
        P(),
        P(),
    )
    out_specs = P("ta", "ha", None)
    return jax.shard_map(shards, mesh=mesh, in_specs=in_specs, out_specs=out_specs, check_vma=False)
```
